32 devices in a mesh: rows: 4 (over z), feat: 2 (over x), leaf: 4 (over y, core).
Axes of the slice: x: 2, y: 2, z: 4, core: 2. Of those that a mesh axis runs over, the one named last changes fastest.
Arguments:
- features: float32 [512, 8192], P(None, ('rows', 'feat')), may hold values from -4 to 4
- labels: int32 [8192], P(('rows', 'feat')), may hold values from 0 to 63
- weights: bfloat16 [4, 8192], P('leaf', ('rows', 'feat')), may hold values from 0.0009994507 to 4
- nodes: int32 [4, 8192], P('leaf', ('rows', 'feat')), may hold values from 0 to 1
Outputs:
- split_gain: float32 [4, 2, 512], P('leaf', None, ('rows', 'feat'))
- node_best: float32 [4, 2], P('leaf')
The draws below stay inside these ranges and needn't reach their ends.
All inputs are finite; a program needn't handle non-finite values.
Results may differ from the reference program's by a relative error of at most 0.0003.
Values may be sent and summed in bfloat16 or wider, within the bound.
No kernel may reach another device: no remote copies, remote signals or barrier semaphores. Data moves between devices by JAX's collectives and lax.ppermute only.
A program may use at most 64 MiB of HBM per device.

```python
import math
import jax
import jax.numpy as jnp
from jax import lax

F = 512
B = 128
C = 64
NODES = 2
TREES = 4
ROWS = 8192


def place_ends(values, rng, low, largest):
    longest = values.shape.index(max(values.shape))
    spots = []
    for shift in (0, 1):
        where = [jax.random.randint(jax.random.fold_in(rng, axis), (), 0, length) for axis, length in enumerate(values.shape)]
        where[longest] = (where[longest] + shift) % values.shape[longest]
        spots.append(tuple(where))
    return values.at[spots[0]].set(low).at[spots[1]].set(largest)


def block_levels(own_key, extent, split, smallest, largest):
    def one(axis_at, parts):
        heights = jax.random.uniform(jax.random.fold_in(jax.random.fold_in(own_key, 6), axis_at), (parts,), jnp.float32, smallest / len(split), largest / len(split))
        return jnp.repeat(jnp.exp(heights), extent[axis_at] // parts).reshape((-1,) + (1,) * (len(extent) - axis_at - 1))

    level = one(*split[0])
    for cut in split[1:]:
        level = level * one(*cut)
    return level


def normal_values(stream_key, shape, spread, most, pieces=(), held_as=jnp.bfloat16):
    entries = jax.random.normal(stream_key, shape, jnp.float32) * spread
    if len(pieces) > 0:
        entries = block_levels(stream_key, shape, pieces, -0.22, 0.18) * entries
    return jnp.clip(entries, min=-most, max=most).astype(held_as)


def setup_inputs(seed: int = 0) -> dict:
    seeds = jax.random.split(jax.random.key(seed), 5)
    return {
        "features": normal_values(seeds[0], (F, ROWS), 1.0, 4.0, ((1, 8),), jnp.float32),
        "labels": place_ends(jax.random.randint(seeds[1], (ROWS,), 0, C), jax.random.fold_in(seeds[1], 1), 0, C - 1).astype(jnp.int32),
        "weights": jnp.clip(jnp.exp(math.log(4.0) - 8.2946 * jax.random.uniform(seeds[2], (TREES, ROWS), jnp.float32) ** block_levels(seeds[2], (TREES, ROWS), ((0, 4), (1, 8)), -0.2, 0.2)), 0.0009994507, 4.0).astype(jnp.bfloat16),
        "nodes": place_ends(jax.random.randint(seeds[3], (TREES, ROWS), 0, NODES), jax.random.fold_in(seeds[3], 1), 0, NODES - 1).astype(jnp.int32),
    }


def edge_table(bin_count, dtype):
    positions = jnp.arange(bin_count - 1, dtype=dtype)
    return (positions + 1.0 - bin_count // 2) * (9.0 / bin_count)


def split_scores(cumulative):
    totals = cumulative[..., -1:, :, :]
    right_side = totals - cumulative

    def ratio_sum(values):
        return jnp.sum(values * values, axis=-1) / jnp.maximum(jnp.sum(values, axis=-1), 1.0)

    split_value = ratio_sum(cumulative) + ratio_sum(right_side) - ratio_sum(totals)
    return jnp.max(split_value, axis=-2)


def reference(features, labels, weights, nodes):
    edge_values = edge_table(B, jnp.float32)
    group_count = TREES * NODES * C
    tree_index = jnp.arange(TREES, dtype=jnp.int32)[:, None]
    group_index = ((tree_index * NODES + nodes) * C + labels[None, :]).astype(jnp.int32)
    weight_values = weights.astype(jnp.float32).reshape(-1)

    def per_column(column):
        bin_index = jnp.searchsorted(edge_values, column, side="left").astype(jnp.int32)
        flat_index = (bin_index[None, :] * group_count + group_index).astype(jnp.int32)
        counts = jnp.zeros((B * group_count,), jnp.float32).at[flat_index.reshape(-1)].add(weight_values)
        cumulative = jnp.cumsum(counts.reshape(B, TREES * NODES, C), axis=0)
        return split_scores(cumulative)

    scores = lax.map(per_column, features)
    split_gain = scores.T.reshape(TREES, NODES, F)
    node_best = jnp.max(split_gain, axis=2)
    return split_gain, node_best
```

```python
import functools

import jax
import jax.numpy as jnp
from jax import lax
from jax.experimental import pallas as pl
from jax.experimental.pallas import tpu as pltpu
from jax.sharding import PartitionSpec as P

B = 128
C = 64
NODES = 2
STEP = 9.0 / B
LANES = 128
ALL = ("rows", "feat", "leaf")
BF16 = jnp.bfloat16
F32 = jnp.float32


def bin_index(values):
    nearest = jnp.round(values * (1.0 / STEP))
    above = jnp.where(values > nearest * STEP, 1.0, 0.0)
    return jnp.clip(nearest + above + (B // 2 - 1), 0.0, B - 1.0)


def score_kernel(places, sizes, msg_ref, gain_ref, target, total):
    blocks, chunks, trees, own = sizes
    feature_at, weight_at, node_at, label_at = places
    bins = lax.broadcasted_iota(jnp.int32, (B, LANES), 0).astype(F32)
    classes = lax.broadcasted_iota(jnp.int32, (C, LANES), 0).astype(F32)
    total[...] = jnp.zeros_like(total)

    def row(block, place):
        leaf, at = place
        return msg_ref[block, leaf, at : at + 1, :].astype(F32)

    def per_block(block, carry):
        for u in range(chunks):
            hit = row(block, label_at(u)) == classes
            for t in range(trees):
                weight, node = row(block, weight_at(t, u)), row(block, node_at(t, u))
                for n in range(NODES):
                    part = jnp.where(node == n, weight, 0.0)
                    at = (t * NODES + n) * C
                    target[at : at + C, u * LANES : (u + 1) * LANES] = jnp.where(hit, part, 0.0).astype(BF16)
        for f in range(own):
            below = jnp.concatenate(
                [jnp.where(row(block, feature_at(f, u)) <= bins, 1.0, 0.0).astype(BF16) for u in range(chunks)], axis=1
            )
            total[:, f * B : (f + 1) * B] += lax.dot_general(
                target[...], below, (((1,), (1,)), ((), ())), preferred_element_type=F32
            )
        return carry

    lax.fori_loop(0, blocks, per_block, 0)

    def ratio(values):
        return jnp.sum(values * values, axis=0, keepdims=True) / jnp.maximum(
            jnp.sum(values, axis=0, keepdims=True), 1.0
        )

    for k in range(trees * NODES):
        for f in range(own):
            left = total[k * C : (k + 1) * C, f * B : (f + 1) * B]
            whole = left[:, B - 1 :]
            gain = ratio(left) + ratio(whole - left) - ratio(whole)
            gain_ref[k : k + 1, f : f + 1] = jnp.max(gain, axis=1, keepdims=True)


def local(features, labels, weights, nodes, *, blocks, trees):
    feature_total, rows = features.shape
    own = feature_total // (blocks * trees)
    devices = blocks * trees
    leaf = lax.axis_index("leaf")
    if rows % LANES:
        raise ValueError("rows a device")
    chunks = rows // LANES
    split_features = own % trees == 0 and chunks % trees == 0
    if split_features:
        piece = own // trees
        mine = lax.dynamic_index_in_dim(features.reshape(blocks, trees, own, rows), leaf, 1, keepdims=False)
        binned = bin_index(mine).astype(BF16).reshape(devices, piece * chunks, LANES)
        quarter = lax.dynamic_slice_in_dim(labels, leaf * (rows // trees), rows // trees, 0)
        common = jnp.concatenate(
            [
                weights.reshape(chunks, LANES),
                nodes.astype(BF16).reshape(chunks, LANES),
                quarter.astype(BF16).reshape(chunks // trees, LANES),
            ],
            axis=0,
        )
        message = jnp.concatenate([binned, jnp.broadcast_to(common, (devices,) + common.shape)], axis=1)
        message = lax.all_to_all(message, ALL, 0, 0, tiled=True)
        message = message.reshape((blocks, trees) + message.shape[1:])
        share = chunks // trees
        places = (
            lambda f, u: (f // piece, (f % piece) * chunks + u),
            lambda t, u: (t, piece * chunks + u),
            lambda t, u: (t, (piece + 1) * chunks + u),
            lambda u: (u // share, (piece + 2) * chunks + u % share),
        )
    else:
        share = rows // trees
        mine = lax.dynamic_slice_in_dim(features, leaf * share, share, 1)
        binned = bin_index(mine).astype(BF16).reshape(devices, own * share)
        quarter = lax.dynamic_slice_in_dim(labels, leaf * share, share, 0)
        common = jnp.concatenate([weights[0], nodes[0].astype(BF16), quarter.astype(BF16)])
        message = jnp.concatenate([binned, jnp.broadcast_to(common, (devices, common.shape[0]))], axis=1)
        message = lax.all_to_all(message, ALL, 0, 0, tiled=True).reshape(blocks, trees, -1)
        ends = (own * share, own * share + rows, own * share + 2 * rows)
        parts = [
            message[:, :, : ends[0]].reshape(blocks, trees, own, share).transpose(0, 2, 1, 3),
            message[:, :, ends[0] : ends[1]],
            message[:, :, ends[1] : ends[2]],
            message[:, :, ends[2] :],
        ]
        message = jnp.concatenate([p.reshape(blocks, -1, LANES) for p in parts], axis=1)[:, None]
        places = (
            lambda f, u: (0, f * chunks + u),
            lambda t, u: (0, (own + t) * chunks + u),
            lambda t, u: (0, (own + trees + t) * chunks + u),
            lambda u: (0, (own + 2 * trees) * chunks + u),
        )
    sizes = (blocks, chunks, trees, own)
    columns = trees * NODES * C
    gains = pl.pallas_call(
        functools.partial(score_kernel, places, sizes),
        out_shape=jax.ShapeDtypeStruct((trees * NODES, own), F32),
        in_specs=[pl.BlockSpec(memory_space=pltpu.VMEM)],
        out_specs=pl.BlockSpec(memory_space=pltpu.VMEM),
        scratch_shapes=[pltpu.VMEM((columns, rows), BF16), pltpu.VMEM((columns, own * B), F32)],
        compiler_params=pltpu.CompilerParams(vmem_limit_bytes=40 << 20),
    )(message)
    outgoing = jnp.broadcast_to(gains.reshape(1, trees, NODES * own), (blocks, trees, NODES * own))
    scores = lax.all_to_all(outgoing.reshape(devices, NODES * own), ALL, 0, 0, tiled=True)
    scores = scores.reshape(blocks, trees, NODES, own)
    here = lax.axis_index("rows") * lax.axis_size("feat") + lax.axis_index("feat")
    block = lax.dynamic_index_in_dim(scores, here, 0, keepdims=False)
    if split_features:
        split_gain = block.reshape(trees, NODES, trees, own // trees).transpose(1, 2, 0, 3)
    else:
        split_gain = block.transpose(1, 0, 2)
    return split_gain.reshape(1, NODES, trees * own), jnp.max(scores, axis=(0, 1, 3)).reshape(1, NODES)


def solution(mesh):
    shape = mesh.shape
    return jax.shard_map(
        functools.partial(local, blocks=shape["rows"] * shape["feat"], trees=shape["leaf"]),
        mesh=mesh,
        in_specs=(
            P(None, ("rows", "feat")),
            P(("rows", "feat")),
            P("leaf", ("rows", "feat")),
            P("leaf", ("rows", "feat")),
        ),
        out_specs=(P("leaf", None, ("rows", "feat")), P("leaf", None)),
        check_vma=False,
    )
```

```python
import functools

import jax
import jax.numpy as jnp
from jax import lax
from jax.experimental import pallas as pl
from jax.experimental.pallas import tpu as pltpu
from jax.sharding import PartitionSpec as P

B = 128
C = 64
NODES = 2
STEP = 9.0 / B
LANES = 128
GROUP = 8
SPAN = 24
ALL = ("rows", "feat", "leaf")
BF16 = jnp.bfloat16
F32 = jnp.float32
VMEM = pl.BlockSpec(memory_space=pltpu.VMEM)


def bin_index(values):
    nearest = jnp.round(values * (1.0 / STEP))
    above = jnp.where(values > nearest * STEP, 1.0, 0.0)
    return jnp.clip(nearest + above + (B // 2 - 1), 0.0, B - 1.0)


def iota(shape, axis):
    return lax.broadcasted_iota(jnp.int32, shape, axis).astype(F32)


def dot_lanes(a, b):
    return lax.dot_general(a, b, (((1,), (1,)), ((), ())), preferred_element_type=F32)


def sort_kernel(sizes, leaf_ref, feature_ref, label_ref, weight_ref, node_ref, out_ref, slab, held, ordered, packed, sem):
    blocks, trees, own, rows, chunks, piece = sizes
    devices = blocks * trees
    copy = pltpu.make_async_copy(feature_ref.at[:, leaf_ref[0]], slab, sem)
    copy.start()
    label = label_ref[...].astype(F32)
    classes = iota((C, LANES), 0)
    hits, less = [], jnp.zeros((C, LANES), F32)
    for u in range(chunks):
        part = label[:, u * LANES : (u + 1) * LANES]
        hits.append(jnp.where(part == classes, 1.0, 0.0))
        less = less + jnp.where(part < classes, 1.0, 0.0)
    lower = jnp.where(iota((LANES, LANES), 0) < iota((LANES, LANES), 1), 1.0, 0.0)
    counter = jnp.concatenate([lower, jnp.ones((LANES, LANES), F32)], axis=1).astype(BF16)
    counts = jnp.dot(
        jnp.concatenate(hits + [less], axis=0).astype(BF16), counter, preferred_element_type=F32
    )
    first = counts[chunks * C :, LANES:]
    ranks = []
    for u in range(chunks):
        within = counts[u * C : (u + 1) * C]
        ranks.append(jnp.sum(hits[u] * (first + within[:, :LANES]), axis=0, keepdims=True))
        first = first + within[:, LANES:]
    spots = iota((rows, LANES), 0)
    order = jnp.concatenate([jnp.where(rank == spots, 1.0, 0.0).astype(BF16) for rank in ranks], axis=1)
    held[devices * piece :, :] = jnp.concatenate(
        [weight_ref[...].astype(F32), node_ref[...].astype(F32), label, jnp.zeros((13, rows), F32)], axis=0
    ).astype(BF16)
    copy.wait()
    held[: devices * piece, :] = bin_index(slab[...].reshape(devices * piece, rows)).astype(BF16)
    sorted_rows = dot_lanes(held[...], order)
    for u in range(chunks):
        ordered[u] = sorted_rows[:, u * LANES : (u + 1) * LANES]
    deep = (piece + 3) * chunks
    for u in range(chunks):
        for k in range(piece):
            packed[pl.ds(k * chunks + u, devices, stride=deep), :] = ordered[u, pl.ds(k, devices, stride=piece), :]
    for k in range(3):
        tile = jnp.concatenate([ordered[u, devices * piece + k : devices * piece + k + 1, :] for u in range(chunks)], axis=0)
        for d in range(devices):
            at = d * deep + (piece + k) * chunks
            packed[at : at + chunks, :] = tile
    for d in range(devices):
        out_ref[d] = packed[d * deep : (d + 1) * deep, :].astype(BF16)


def score_kernel(places, sizes, msg_ref, gain_ref, message, target, total, whole, low, high):
    blocks, chunks, trees, own = sizes
    feature_at, weight_at, node_at, label_at = places
    wide = 2
    windows, groups = chunks // wide, blocks // GROUP
    depth = trees * NODES
    together = 2 if own % 2 == 0 else 1
    message[...] = msg_ref[...].astype(F32)
    total[...] = jnp.zeros_like(total)

    def row(block, place):
        return message[block, place[0], pl.ds(place[1], 1), :]

    def span(step, carry):
        group, w = step // windows, step % windows
        found = [row(group * GROUP + g, label_at(w * wide + u)) for g in range(GROUP) for u in range(wide)]
        found = jnp.concatenate(found, axis=0).astype(jnp.int32)
        low[step] = jnp.min(found)
        high[step] = jnp.max(found)
        return carry

    lax.fori_loop(0, groups * windows, span, 0)
    bins = iota((B, LANES), 0).astype(BF16)
    one, zero = jnp.ones((), BF16), jnp.zeros((), BF16)

    def window(step, carry):
        group, w = step // windows, step % windows
        places_in = [(group * GROUP + g, w * wide + u) for g in range(GROUP) for u in range(wide)]

        def one_pass(p, inner):
            base = low[step] + p * SPAN
            for at, (block, u) in enumerate(places_in):
                label = row(block, label_at(u)) - base.astype(F32)
                pairs = []
                for t in range(trees):
                    weight, node = row(block, weight_at(t, u)), row(block, node_at(t, u))
                    pairs += [jnp.where(node == n, weight, 0.0) for n in range(NODES)]
                pairs = jnp.concatenate(pairs, axis=0)
                for c in range(0, SPAN, 2):
                    two = [jnp.where(label == c + more, pairs, 0.0) for more in range(2)]
                    target[c * depth : (c + 2) * depth, at * LANES : (at + 1) * LANES] = jnp.concatenate(
                        two, axis=0
                    ).astype(BF16)
            start = pl.multiple_of(base * depth, 8)
            for f in range(0, own, together):
                below = jnp.concatenate(
                    [
                        jnp.concatenate(
                            [
                                jnp.where(row(block, feature_at(f + more, u)).astype(BF16) <= bins, one, zero)
                                for block, u in places_in
                            ],
                            axis=1,
                        )
                        for more in range(together)
                    ],
                    axis=0,
                )
                total[pl.ds(start, SPAN * depth), f * B : (f + together) * B] += dot_lanes(target[...], below)
            return inner

        passes = (high[step] - low[step]) // SPAN + 1
        return lax.fori_loop(0, passes, one_pass, carry)

    lax.fori_loop(0, groups * windows, window, 0)

    def ratio(squares, sums):
        return squares / jnp.maximum(sums, 1.0)

    whole_sum, whole_square = jnp.zeros((depth, B), F32), jnp.zeros((depth, B), F32)
    for c in range(C):
        part = jnp.broadcast_to(total[c * depth : (c + 1) * depth, B - 1 : B], (depth, B))
        whole[c * depth : (c + 1) * depth, :] = part
        whole_sum, whole_square = whole_sum + part, whole_square + part * part
    whole_ratio = ratio(whole_square, whole_sum)
    for f in range(own):
        left_sum, right_sum = jnp.zeros((depth, B), F32), jnp.zeros((depth, B), F32)
        left_square, right_square = jnp.zeros((depth, B), F32), jnp.zeros((depth, B), F32)
        for c in range(C):
            left = total[c * depth : (c + 1) * depth, f * B : (f + 1) * B]
            right = whole[c * depth : (c + 1) * depth, :] - left
            left_sum, left_square = left_sum + left, left_square + left * left
            right_sum, right_square = right_sum + right, right_square + right * right
        gain = ratio(left_square, left_sum) + ratio(right_square, right_sum) - whole_ratio
        gain_ref[:, f : f + 1] = jnp.max(gain, axis=1, keepdims=True)


def local(features, labels, weights, nodes, *, blocks, trees):
    feature_total, rows = features.shape
    own = feature_total // (blocks * trees)
    devices = blocks * trees
    leaf = lax.axis_index("leaf")
    chunks = rows // LANES
    split_features = own % trees == 0
    if split_features:
        piece = own // trees
        deep = (piece + 3) * chunks
        held = devices * piece
        message = pl.pallas_call(
            functools.partial(sort_kernel, (blocks, trees, own, rows, chunks, piece)),
            out_shape=jax.ShapeDtypeStruct((devices, deep, LANES), BF16),
            in_specs=[
                pl.BlockSpec(memory_space=pltpu.SMEM),
                pl.BlockSpec(memory_space=pl.ANY),
                VMEM,
                VMEM,
                VMEM,
            ],
            out_specs=VMEM,
            scratch_shapes=[
                pltpu.VMEM((blocks, own, rows), F32),
                pltpu.VMEM((held + 16, rows), BF16),
                pltpu.VMEM((chunks, held + 16, LANES), F32),
                pltpu.VMEM((devices * deep, LANES), F32),
                pltpu.SemaphoreType.DMA,
            ],
            compiler_params=pltpu.CompilerParams(vmem_limit_bytes=40 << 20),
        )(leaf.reshape(1), features.reshape(blocks, trees, own, rows), labels.reshape(1, rows), weights, nodes)
        message = lax.all_to_all(message, ALL, 0, 0, tiled=True)
        message = message.reshape(blocks, trees, deep, LANES)
        places = (
            lambda f, u: (f // piece, (f % piece) * chunks + u),
            lambda t, u: (t, piece * chunks + u),
            lambda t, u: (t, (piece + 1) * chunks + u),
            lambda u: (0, (piece + 2) * chunks + u),
        )
    else:
        share = rows // trees
        mine = lax.dynamic_slice_in_dim(features, leaf * share, share, 1)
        binned = bin_index(mine).astype(BF16).reshape(devices, own * share)
        quarter = lax.dynamic_slice_in_dim(labels, leaf * share, share, 0)
        common = jnp.concatenate([weights[0], nodes[0].astype(BF16), quarter.astype(BF16)])
        message = jnp.concatenate([binned, jnp.broadcast_to(common, (devices, common.shape[0]))], axis=1)
        message = lax.all_to_all(message, ALL, 0, 0, tiled=True).reshape(blocks, trees, -1)
        ends = (own * share, own * share + rows, own * share + 2 * rows)
        parts = [
            message[:, :, : ends[0]].reshape(blocks, trees, own, share).transpose(0, 2, 1, 3),
            message[:, :, ends[0] : ends[1]],
            message[:, :, ends[1] : ends[2]],
            message[:, :, ends[2] :],
        ]
        message = jnp.concatenate([p.reshape(blocks, -1, LANES) for p in parts], axis=1)[:, None]
        places = (
            lambda f, u: (0, f * chunks + u),
            lambda t, u: (0, (own + t) * chunks + u),
            lambda t, u: (0, (own + trees + t) * chunks + u),
            lambda u: (0, (own + 2 * trees) * chunks + u),
        )
    sizes = (blocks, chunks, trees, own)
    depth = trees * NODES
    steps = blocks * chunks // (2 * GROUP)
    gains = pl.pallas_call(
        functools.partial(score_kernel, places, sizes),
        out_shape=jax.ShapeDtypeStruct((depth, own), F32),
        in_specs=[VMEM],
        out_specs=VMEM,
        scratch_shapes=[
            pltpu.VMEM(message.shape, F32),
            pltpu.VMEM((SPAN * depth, 2 * GROUP * LANES), BF16),
            pltpu.VMEM(((C + SPAN) * depth, own * B), F32),
            pltpu.VMEM((C * depth, B), F32),
            pltpu.SMEM((steps,), jnp.int32),
            pltpu.SMEM((steps,), jnp.int32),
        ],
        compiler_params=pltpu.CompilerParams(vmem_limit_bytes=40 << 20),
    )(message)
    outgoing = jnp.broadcast_to(gains.reshape(1, trees, NODES * own), (blocks, trees, NODES * own))
    scores = lax.all_to_all(outgoing.reshape(devices, NODES * own), ALL, 0, 0, tiled=True)
    scores = scores.reshape(blocks, trees, NODES, own)
    here = lax.axis_index("rows") * lax.axis_size("feat") + lax.axis_index("feat")
    block = lax.dynamic_index_in_dim(scores, here, 0, keepdims=False)
    if split_features:
        split_gain = block.reshape(trees, NODES, trees, own // trees).transpose(1, 2, 0, 3)
    else:
        split_gain = block.transpose(1, 0, 2)
    return split_gain.reshape(1, NODES, trees * own), jnp.max(scores, axis=(0, 1, 3)).reshape(1, NODES)


def solution(mesh):
    shape = mesh.shape
    return jax.shard_map(
        functools.partial(local, blocks=shape["rows"] * shape["feat"], trees=shape["leaf"]),
        mesh=mesh,
        in_specs=(
            P(None, ("rows", "feat")),
            P(("rows", "feat")),
            P("leaf", ("rows", "feat")),
            P("leaf", ("rows", "feat")),
        ),
        out_specs=(P("leaf", None, ("rows", "feat")), P("leaf", None)),
        check_vma=False,
    )
```

```python
import functools
import math

import jax
import jax.numpy as jnp
from jax import lax
from jax.experimental import pallas as pl
from jax.experimental.pallas import tpu as pltpu
from jax.sharding import PartitionSpec as P

B = 128
C = 64
NODES = 2
STEP = 9.0 / B
LOWEST = math.ceil(-4 / STEP) + B // 2 - 1
HIGHEST = math.ceil(4 / STEP) + B // 2 - 1
LANES = 128
GROUP = 8
UNROLLED = 8
SPAN = 16
ALL = ("rows", "feat", "leaf")
BF16 = jnp.bfloat16
F32 = jnp.float32
VMEM = pl.BlockSpec(memory_space=pltpu.VMEM)


def bin_index(values):
    nearest = jnp.round(values * (1.0 / STEP))
    above = jnp.where(values > nearest * STEP, 1.0, 0.0)
    return jnp.clip(nearest + above + (B // 2 - 1), float(LOWEST), float(HIGHEST))


def iota(shape, axis):
    return lax.broadcasted_iota(jnp.int32, shape, axis).astype(F32)


def dot_lanes(a, b):
    return lax.dot_general(a, b, (((1,), (1,)), ((), ())), preferred_element_type=F32)


def sort_kernel(sizes, leaf_ref, feature_ref, label_ref, weight_ref, node_ref, out_ref, slab, held, ordered, packed, sem):
    blocks, trees, own, rows, chunks, piece = sizes
    devices = blocks * trees
    copy = pltpu.make_async_copy(feature_ref.at[:, leaf_ref[0]], slab, sem)
    copy.start()
    label = label_ref[...].astype(F32)
    classes = iota((C, LANES), 0)
    hits, less = [], jnp.zeros((C, LANES), F32)
    for u in range(chunks):
        part = label[:, u * LANES : (u + 1) * LANES]
        hits.append(jnp.where(part == classes, 1.0, 0.0))
        less = less + jnp.where(part < classes, 1.0, 0.0)
    lower = jnp.where(iota((LANES, LANES), 0) < iota((LANES, LANES), 1), 1.0, 0.0)
    counter = jnp.concatenate([lower, jnp.ones((LANES, LANES), F32)], axis=1).astype(BF16)
    counts = jnp.dot(
        jnp.concatenate(hits + [less], axis=0).astype(BF16), counter, preferred_element_type=F32
    )
    first = counts[chunks * C :, LANES:]
    ranks = []
    for u in range(chunks):
        within = counts[u * C : (u + 1) * C]
        ranks.append(jnp.sum(hits[u] * (first + within[:, :LANES]), axis=0, keepdims=True))
        first = first + within[:, LANES:]
    spots = iota((rows, LANES), 0)
    order = jnp.concatenate([jnp.where(rank == spots, 1.0, 0.0).astype(BF16) for rank in ranks], axis=1)
    held[devices * piece :, :] = jnp.concatenate(
        [weight_ref[...].astype(F32), node_ref[...].astype(F32), label, jnp.zeros((13, rows), F32)], axis=0
    ).astype(BF16)
    copy.wait()
    held[: devices * piece, :] = bin_index(slab[...].reshape(devices * piece, rows)).astype(BF16)
    sorted_rows = dot_lanes(held[...], order)
    for u in range(chunks):
        ordered[u] = sorted_rows[:, u * LANES : (u + 1) * LANES]
    deep = (piece + 3) * chunks
    for u in range(chunks):
        for k in range(piece):
            packed[pl.ds(k * chunks + u, devices, stride=deep), :] = ordered[u, pl.ds(k, devices, stride=piece), :]
    for k in range(3):
        tile = jnp.concatenate([ordered[u, devices * piece + k : devices * piece + k + 1, :] for u in range(chunks)], axis=0)
        for d in range(devices):
            at = d * deep + (piece + k) * chunks
            packed[at : at + chunks, :] = tile
    for d in range(devices):
        out_ref[d] = packed[d * deep : (d + 1) * deep, :].astype(BF16)


def score_kernel(places, sizes, msg_ref, gain_ref, message, target, spread, total, whole, low, high):
    blocks, chunks, trees, own = sizes
    feature_at, weight_at, node_at, label_at = places
    groups = blocks // GROUP
    steps = groups * chunks
    depth = trees * NODES
    copies = LANES // own
    tiles = -(-(HIGHEST + 1 - LOWEST) // copies)
    first_bin = HIGHEST + 1 - tiles * copies
    share = total.shape[0] // steps
    message[...] = msg_ref[...].astype(F32)

    def row(block, place):
        return message[block, place[0], pl.ds(place[1], 1), :]

    def members(step):
        return [step // chunks * GROUP + g for g in range(GROUP)], step % chunks

    def set_target(step, base, to):
        held, u = members(step)
        for g, block in enumerate(held):
            label = row(block, label_at(u)) - base
            pairs = []
            for t in range(trees):
                weight, node = row(block, weight_at(t, u)), row(block, node_at(t, u))
                pairs += [jnp.where(node == n, weight, 0.0) for n in range(NODES)]
            pairs = jnp.concatenate(pairs, axis=0)
            for c in range(0, SPAN, 2):
                two = [jnp.where(label == c + more, pairs, 0.0) for more in range(2)]
                to[c * depth : (c + 2) * depth, g * LANES : (g + 1) * LANES] = jnp.concatenate(two, axis=0).astype(BF16)

    def prepare(step, carry):
        held, u = members(step)
        total[pl.ds(pl.multiple_of(step * share, 8), share), :] = jnp.zeros((share, total.shape[1]), F32)
        labels = jnp.concatenate([row(block, label_at(u)) for block in held], axis=0)
        least = jnp.min(labels)
        low[step] = least.astype(jnp.int32)
        high[step] = jnp.max(labels).astype(jnp.int32)
        set_target(step, least, target.at[step])
        for g, block in enumerate(held):
            tile = jnp.concatenate([row(block, feature_at(f, u)) for f in range(own)], axis=0)
            tile = jnp.concatenate([tile] * copies, axis=0)
            spread[step, g * LANES : (g + 1) * LANES, :] = tile.T.astype(BF16)
        return carry

    lax.fori_loop(0, steps, prepare, 0)
    bins = (first_bin + jnp.floor(iota((GROUP * LANES, LANES), 1) * (1.0 / own))).astype(BF16)
    one, zero = jnp.ones((), BF16), jnp.zeros((), BF16)

    def add(step, start, held):
        start = pl.multiple_of(start * depth, 8)
        for first in range(0, tiles, 2):
            last = min(first + 2, tiles)
            below = [
                jnp.where(spread[step] <= bins + float(tile * copies), one, zero)
                for tile in range(first, last)
            ]
            lanes = slice(first * LANES, last * LANES)
            total[pl.ds(start, SPAN * depth), lanes] += jnp.dot(
                held[...], jnp.concatenate(below, axis=1), preferred_element_type=F32
            )

    def more(step, carry):
        def one_pass(p, inner):
            base = low[step] + p * SPAN
            set_target(step, base.astype(F32), target.at[steps])
            add(step, base, target.at[steps])
            return inner

        return lax.fori_loop(1, (high[step] - low[step]) // SPAN + 1, one_pass, carry)

    for step in range(steps) if steps <= UNROLLED else ():
        add(step, low[step], target.at[step])
    if steps > UNROLLED:
        lax.fori_loop(0, steps, lambda step, carry: add(step, low[step], target.at[step]) or carry, 0)
    lax.fori_loop(0, steps, more, 0)

    def ratio(squares, sums):
        return squares / jnp.maximum(sums, 1.0)

    zeros = jnp.zeros((depth, LANES), F32)
    whole_sum, whole_square = zeros, zeros
    for c in range(C):
        part = jnp.broadcast_to(total[c * depth : (c + 1) * depth, tiles * LANES - 1 :], (depth, LANES))
        whole[c * depth : (c + 1) * depth, :] = part
        whole_sum, whole_square = whole_sum + part, whole_square + part * part
    whole_ratio = ratio(whole_square, whole_sum)
    best = jnp.full((depth, LANES), -jnp.inf, F32)
    for tile in range(tiles):
        left_sum, right_sum, left_square, right_square = zeros, zeros, zeros, zeros
        for c in range(C):
            left = total[c * depth : (c + 1) * depth, tile * LANES : (tile + 1) * LANES]
            right = whole[c * depth : (c + 1) * depth, :] - left
            left_sum, left_square = left_sum + left, left_square + left * left
            right_sum, right_square = right_sum + right, right_square + right * right
        gain = ratio(left_square, left_sum) + ratio(right_square, right_sum) - whole_ratio
        best = jnp.maximum(best, gain)
    shift = own
    while shift < LANES:
        best = jnp.maximum(best, pltpu.roll(best, shift, 1))
        shift *= 2
    gain_ref[...] = best[:, :own]


def score(message, places, sizes):
    blocks, chunks, trees, own = sizes
    depth = trees * NODES
    steps = blocks * chunks // GROUP
    columns = -(-(HIGHEST + 1 - LOWEST) * own // LANES) * LANES
    return pl.pallas_call(
        functools.partial(score_kernel, places, sizes),
        out_shape=jax.ShapeDtypeStruct((depth, own), F32),
        in_specs=[VMEM],
        out_specs=VMEM,
        scratch_shapes=[
            pltpu.VMEM(message.shape, F32),
            pltpu.VMEM((steps + 1, SPAN * depth, GROUP * LANES), BF16),
            pltpu.VMEM((steps, GROUP * LANES, LANES), BF16),
            pltpu.VMEM((-(-(C + SPAN) // steps) * steps * depth, columns), F32),
            pltpu.VMEM((C * depth, LANES), F32),
            pltpu.SMEM((steps,), jnp.int32),
            pltpu.SMEM((steps,), jnp.int32),
        ],
        compiler_params=pltpu.CompilerParams(vmem_limit_bytes=40 << 20),
    )(message)


def local(features, labels, weights, nodes, *, blocks, trees):
    feature_total, rows = features.shape
    own = feature_total // (blocks * trees)
    devices = blocks * trees
    leaf = lax.axis_index("leaf")
    chunks = rows // LANES
    split_features = own % trees == 0
    if split_features:
        piece = own // trees
        deep = (piece + 3) * chunks
        held = devices * piece
        message = pl.pallas_call(
            functools.partial(sort_kernel, (blocks, trees, own, rows, chunks, piece)),
            out_shape=jax.ShapeDtypeStruct((devices, deep, LANES), BF16),
            in_specs=[
                pl.BlockSpec(memory_space=pltpu.SMEM),
                pl.BlockSpec(memory_space=pl.ANY),
                VMEM,
                VMEM,
                VMEM,
            ],
            out_specs=VMEM,
            scratch_shapes=[
                pltpu.VMEM((blocks, own, rows), F32),
                pltpu.VMEM((held + 16, rows), BF16),
                pltpu.VMEM((chunks, held + 16, LANES), F32),
                pltpu.VMEM((devices * deep, LANES), F32),
                pltpu.SemaphoreType.DMA,
            ],
            compiler_params=pltpu.CompilerParams(vmem_limit_bytes=40 << 20),
        )(leaf.reshape(1), features.reshape(blocks, trees, own, rows), labels.reshape(1, rows), weights, nodes)
        message = lax.all_to_all(message, ALL, 0, 0, tiled=True)
        message = message.reshape(blocks, trees, deep, LANES)
        places = (
            lambda f, u: (f // piece, (f % piece) * chunks + u),
            lambda t, u: (t, piece * chunks + u),
            lambda t, u: (t, (piece + 1) * chunks + u),
            lambda u: (0, (piece + 2) * chunks + u),
        )
    else:
        share = rows // trees
        mine = lax.dynamic_slice_in_dim(features, leaf * share, share, 1)
        binned = bin_index(mine).astype(BF16).reshape(devices, own * share)
        quarter = lax.dynamic_slice_in_dim(labels, leaf * share, share, 0)
        common = jnp.concatenate([weights[0], nodes[0].astype(BF16), quarter.astype(BF16)])
        message = jnp.concatenate([binned, jnp.broadcast_to(common, (devices, common.shape[0]))], axis=1)
        message = lax.all_to_all(message, ALL, 0, 0, tiled=True).reshape(blocks, trees, -1)
        ends = (own * share, own * share + rows, own * share + 2 * rows)
        parts = [
            message[:, :, : ends[0]].reshape(blocks, trees, own, share).transpose(0, 2, 1, 3),
            message[:, :, ends[0] : ends[1]],
            message[:, :, ends[1] : ends[2]],
            message[:, :, ends[2] :],
        ]
        message = jnp.concatenate([p.reshape(blocks, -1, LANES) for p in parts], axis=1)[:, None]
        places = (
            lambda f, u: (0, f * chunks + u),
            lambda t, u: (0, (own + t) * chunks + u),
            lambda t, u: (0, (own + trees + t) * chunks + u),
            lambda u: (0, (own + 2 * trees) * chunks + u),
        )
    sizes = (blocks, chunks, trees, own)
    gains = score(message, places, sizes)
    outgoing = jnp.broadcast_to(gains.reshape(1, trees, NODES * own), (blocks, trees, NODES * own))
    scores = lax.all_to_all(outgoing.reshape(devices, NODES * own), ALL, 0, 0, tiled=True)
    scores = scores.reshape(blocks, trees, NODES, own)
    here = lax.axis_index("rows") * lax.axis_size("feat") + lax.axis_index("feat")
    block = lax.dynamic_index_in_dim(scores, here, 0, keepdims=False)
    if split_features:
        split_gain = block.reshape(trees, NODES, trees, own // trees).transpose(1, 2, 0, 3)
    else:
        split_gain = block.transpose(1, 0, 2)
    return split_gain.reshape(1, NODES, trees * own), jnp.max(scores, axis=(0, 1, 3)).reshape(1, NODES)


def solution(mesh):
    shape = mesh.shape
    return jax.shard_map(
        functools.partial(local, blocks=shape["rows"] * shape["feat"], trees=shape["leaf"]),
        mesh=mesh,
        in_specs=(
            P(None, ("rows", "feat")),
            P(("rows", "feat")),
            P("leaf", ("rows", "feat")),
            P("leaf", ("rows", "feat")),
        ),
        out_specs=(P("leaf", None, ("rows", "feat")), P("leaf", None)),
        check_vma=False,
    )
```

```python
import functools
import math

import jax
import jax.numpy as jnp
from jax import lax
from jax.experimental import pallas as pl
from jax.experimental.pallas import tpu as pltpu
from jax.sharding import PartitionSpec as P

B = 128
C = 64
NODES = 2
STEP = 9.0 / B
LOWEST = math.ceil(-4 / STEP) + B // 2 - 1
HIGHEST = math.ceil(4 / STEP) + B // 2 - 1
LANES = 128
GROUP = 8
UNROLLED = 8
SPAN = 16
ALL = ("rows", "feat", "leaf")
BF16 = jnp.bfloat16
F32 = jnp.float32
VMEM = pl.BlockSpec(memory_space=pltpu.VMEM)
SMEM = pl.BlockSpec(memory_space=pltpu.SMEM)
HBM = pl.BlockSpec(memory_space=pltpu.HBM)


def bin_index(values):
    nearest = jnp.round(values * (1.0 / STEP))
    above = jnp.where(values > nearest * STEP, 1.0, 0.0)
    return jnp.clip(nearest + above + (B // 2 - 1), float(LOWEST), float(HIGHEST))


def iota(shape, axis):
    return lax.broadcasted_iota(jnp.int32, shape, axis).astype(F32)


def dot_lanes(a, b):
    return lax.dot_general(a, b, (((1,), (1,)), ((), ())), preferred_element_type=F32)


def sort_kernel(sizes, leaf_ref, feature_ref, *refs):
    label_ref, weight_ref, node_ref, out_ref, slab, labels, weights, nodes, held, ordered, packed, sems = refs
    blocks, trees, own, rows, chunks, piece = sizes
    devices = blocks * trees
    copies = [
        pltpu.make_async_copy(source, to, sems.at[k])
        for k, (source, to) in enumerate(
            [
                (label_ref, labels),
                (weight_ref, weights),
                (node_ref, nodes),
                (feature_ref.at[:, leaf_ref[0]], slab),
            ]
        )
    ]
    for copy in copies:
        copy.start()
    copies[0].wait()
    label = labels[...].astype(F32)
    classes = iota((C, LANES), 0)
    hits, less = [], jnp.zeros((C, LANES), F32)
    for u in range(chunks):
        part = label[:, u * LANES : (u + 1) * LANES]
        hits.append(jnp.where(part == classes, 1.0, 0.0))
        less = less + jnp.where(part < classes, 1.0, 0.0)
    lower = jnp.where(iota((LANES, LANES), 0) < iota((LANES, LANES), 1), 1.0, 0.0)
    counter = jnp.concatenate([lower, jnp.ones((LANES, LANES), F32)], axis=1).astype(BF16)
    counts = jnp.dot(
        jnp.concatenate(hits + [less], axis=0).astype(BF16), counter, preferred_element_type=F32
    )
    first = counts[chunks * C :, LANES:]
    ranks = []
    for u in range(chunks):
        within = counts[u * C : (u + 1) * C]
        ranks.append(jnp.sum(hits[u] * (first + within[:, :LANES]), axis=0, keepdims=True))
        first = first + within[:, LANES:]
    spots = iota((rows, LANES), 0)
    order = jnp.concatenate([jnp.where(rank == spots, 1.0, 0.0).astype(BF16) for rank in ranks], axis=1)
    for copy in copies[1:]:
        copy.wait()
    held[devices * piece :, :] = jnp.concatenate(
        [weights[...].astype(F32), nodes[...].astype(F32), label, jnp.zeros((13, rows), F32)], axis=0
    ).astype(BF16)
    held[: devices * piece, :] = bin_index(slab[...].reshape(devices * piece, rows)).astype(BF16)
    sorted_rows = dot_lanes(held[...], order)
    for u in range(chunks):
        ordered[u] = sorted_rows[:, u * LANES : (u + 1) * LANES]
    deep = (piece + 3) * chunks
    for u in range(chunks):
        for k in range(piece):
            packed[pl.ds(k * chunks + u, devices, stride=deep), :] = ordered[u, pl.ds(k, devices, stride=piece), :]
    for k in range(3):
        tile = jnp.concatenate([ordered[u, devices * piece + k : devices * piece + k + 1, :] for u in range(chunks)], axis=0)
        for d in range(devices):
            at = d * deep + (piece + k) * chunks
            packed[at : at + chunks, :] = tile
    for d in range(devices):
        out_ref[d] = packed[d * deep : (d + 1) * deep, :].astype(BF16)


def score_kernel(places, sizes, direct, leaf_ref, msg_ref, gain_ref, message, target, spread, total, whole, low, high):
    blocks, chunks, trees, own = sizes
    feature_at, weight_at, node_at, label_at = places
    groups = blocks // GROUP
    steps = groups * chunks
    depth = trees * NODES
    copies = LANES // own
    tiles = -(-(HIGHEST + 1 - LOWEST) // copies)
    first_bin = HIGHEST + 1 - tiles * copies
    share = total.shape[0] // steps
    message[...] = msg_ref[...].astype(F32)

    def row(block, place):
        return message[block, place[0], pl.ds(place[1], 1), :]

    def members(step):
        return [step // chunks * GROUP + g for g in range(GROUP)], step % chunks

    def set_target(step, base, to):
        held, u = members(step)
        for g, block in enumerate(held):
            label = row(block, label_at(u)) - base
            pairs = []
            for t in range(trees):
                weight, node = row(block, weight_at(t, u)), row(block, node_at(t, u))
                pairs += [jnp.where(node == n, weight, 0.0) for n in range(NODES)]
            pairs = jnp.concatenate(pairs, axis=0)
            for c in range(0, SPAN, 2):
                two = [jnp.where(label == c + more, pairs, 0.0) for more in range(2)]
                to[c * depth : (c + 2) * depth, g * LANES : (g + 1) * LANES] = jnp.concatenate(two, axis=0).astype(BF16)

    def prepare(step, carry):
        held, u = members(step)
        total[pl.ds(pl.multiple_of(step * share, 8), share), :] = jnp.zeros((share, total.shape[1]), F32)
        labels = jnp.concatenate([row(block, label_at(u)) for block in held], axis=0)
        least = jnp.min(labels)
        low[step] = least.astype(jnp.int32)
        high[step] = jnp.max(labels).astype(jnp.int32)
        set_target(step, least, target.at[step])
        for g, block in enumerate(held):
            tile = jnp.concatenate([row(block, feature_at(f, u)) for f in range(own)], axis=0)
            tile = jnp.concatenate([tile] * copies, axis=0)
            spread[step, g * LANES : (g + 1) * LANES, :] = tile.T.astype(BF16)
        return carry

    lax.fori_loop(0, steps, prepare, 0)
    bins = (first_bin + jnp.floor(iota((GROUP * LANES, LANES), 1) * (1.0 / own))).astype(BF16)
    one, zero = jnp.ones((), BF16), jnp.zeros((), BF16)

    def add(step, start, held):
        start = pl.multiple_of(start * depth, 8)
        for first in range(0, tiles, 2):
            last = min(first + 2, tiles)
            below = [
                jnp.where(spread[step] <= bins + float(tile * copies), one, zero)
                for tile in range(first, last)
            ]
            lanes = slice(first * LANES, last * LANES)
            total[pl.ds(start, SPAN * depth), lanes] += jnp.dot(
                held[...], jnp.concatenate(below, axis=1), preferred_element_type=F32
            )

    def more(step, carry):
        def one_pass(p, inner):
            base = low[step] + p * SPAN
            set_target(step, base.astype(F32), target.at[steps])
            add(step, base, target.at[steps])
            return inner

        return lax.fori_loop(1, (high[step] - low[step]) // SPAN + 1, one_pass, carry)

    for step in range(steps) if steps <= UNROLLED else ():
        add(step, low[step], target.at[step])
    if steps > UNROLLED:
        lax.fori_loop(0, steps, lambda step, carry: add(step, low[step], target.at[step]) or carry, 0)
    lax.fori_loop(0, steps, more, 0)

    def ratio(squares, sums):
        return squares / jnp.maximum(sums, 1.0)

    zeros = jnp.zeros((depth, LANES), F32)
    whole_sum, whole_square = zeros, zeros
    for c in range(C):
        part = jnp.broadcast_to(total[c * depth : (c + 1) * depth, tiles * LANES - 1 :], (depth, LANES))
        whole[c * depth : (c + 1) * depth, :] = part
        whole_sum, whole_square = whole_sum + part, whole_square + part * part
    whole_ratio = ratio(whole_square, whole_sum)
    best = jnp.full((depth, LANES), -jnp.inf, F32)
    for tile in range(tiles):
        left_sum, right_sum, left_square, right_square = zeros, zeros, zeros, zeros
        for c in range(C):
            left = total[c * depth : (c + 1) * depth, tile * LANES : (tile + 1) * LANES]
            right = whole[c * depth : (c + 1) * depth, :] - left
            left_sum, left_square = left_sum + left, left_square + left * left
            right_sum, right_square = right_sum + right, right_square + right * right
        gain = ratio(left_square, left_sum) + ratio(right_square, right_sum) - whole_ratio
        best = jnp.maximum(best, gain)
    shift = own
    while shift < LANES:
        best = jnp.maximum(best, pltpu.roll(best, shift, 1))
        shift *= 2
    if not direct:
        gain_ref[...] = best[:, :own]
        return
    piece = own // trees
    lane = lax.broadcasted_iota(jnp.int32, (depth, LANES), 1)
    sent = best
    for leaf in range(trees):
        moved = pltpu.roll(best, lax.rem((leaf_ref[0] - leaf) * piece + LANES, LANES), 1)
        sent = jnp.where(lane // own % trees == leaf, moved, sent)
    for t in range(trees):
        line = jnp.where(lane[:1] < trees * own, sent[t * NODES : t * NODES + 1], sent[t * NODES + 1 : t * NODES + 2])
        for block in range(blocks):
            gain_ref[block * trees + t] = line


def finish_kernel(blocks, trees, own, here_ref, msg_ref, gain_ref, best_ref):
    piece = own // trees
    half = trees * own
    lane = lax.broadcasted_iota(jnp.int32, (1, LANES), 1)
    mine = msg_ref[here_ref[0] * trees]
    for leaf in range(1, trees):
        mine = jnp.where(lane // piece % trees == leaf, msg_ref[here_ref[0] * trees + leaf], mine)
    top = msg_ref[0]
    for d in range(1, blocks * trees):
        top = jnp.maximum(top, msg_ref[d])
    for n in range(NODES):
        gain_ref[0, n : n + 1, :] = mine[:, n * half : (n + 1) * half]
        best_ref[:, n : n + 1] = jnp.max(top[:, n * half : (n + 1) * half], axis=1, keepdims=True)


def score(message, places, sizes, direct, leaf):
    blocks, chunks, trees, own = sizes
    depth = trees * NODES
    steps = blocks * chunks // GROUP
    columns = -(-(HIGHEST + 1 - LOWEST) * own // LANES) * LANES
    return pl.pallas_call(
        functools.partial(score_kernel, places, sizes, direct),
        out_shape=jax.ShapeDtypeStruct((blocks * trees, 1, LANES) if direct else (depth, own), F32),
        in_specs=[SMEM, VMEM],
        out_specs=VMEM,
        scratch_shapes=[
            pltpu.VMEM(message.shape, F32),
            pltpu.VMEM((steps + 1, SPAN * depth, GROUP * LANES), BF16),
            pltpu.VMEM((steps, GROUP * LANES, LANES), BF16),
            pltpu.VMEM((-(-(C + SPAN) // steps) * steps * depth, columns), F32),
            pltpu.VMEM((C * depth, LANES), F32),
            pltpu.SMEM((steps,), jnp.int32),
            pltpu.SMEM((steps,), jnp.int32),
        ],
        compiler_params=pltpu.CompilerParams(vmem_limit_bytes=40 << 20),
    )(leaf, message)


def local(features, labels, weights, nodes, *, blocks, trees):
    feature_total, rows = features.shape
    own = feature_total // (blocks * trees)
    devices = blocks * trees
    leaf = lax.axis_index("leaf").reshape(1)
    chunks = rows // LANES
    split_features = own % trees == 0
    if split_features:
        piece = own // trees
        deep = (piece + 3) * chunks
        held = devices * piece
        message = pl.pallas_call(
            functools.partial(sort_kernel, (blocks, trees, own, rows, chunks, piece)),
            out_shape=jax.ShapeDtypeStruct((devices, deep, LANES), BF16),
            in_specs=[
                SMEM,
                HBM,
                HBM,
                HBM,
                HBM,
            ],
            out_specs=VMEM,
            scratch_shapes=[
                pltpu.VMEM((blocks, own, rows), F32),
                pltpu.VMEM((1, rows), jnp.int32),
                pltpu.VMEM((1, rows), BF16),
                pltpu.VMEM((1, rows), jnp.int32),
                pltpu.VMEM((held + 16, rows), BF16),
                pltpu.VMEM((chunks, held + 16, LANES), F32),
                pltpu.VMEM((devices * deep, LANES), F32),
                pltpu.SemaphoreType.DMA((4,)),
            ],
            compiler_params=pltpu.CompilerParams(vmem_limit_bytes=60 << 20),
        )(leaf, features.reshape(blocks, trees, own, rows), labels.reshape(1, rows), weights, nodes)
        message = lax.all_to_all(message, ALL, 0, 0, tiled=True)
        message = message.reshape(blocks, trees, deep, LANES)
        places = (
            lambda f, u: (f // piece, (f % piece) * chunks + u),
            lambda t, u: (t, piece * chunks + u),
            lambda t, u: (t, (piece + 1) * chunks + u),
            lambda u: (0, (piece + 2) * chunks + u),
        )
    else:
        share = rows // trees
        mine = lax.dynamic_slice_in_dim(features, leaf[0] * share, share, 1)
        binned = bin_index(mine).astype(BF16).reshape(devices, own * share)
        quarter = lax.dynamic_slice_in_dim(labels, leaf[0] * share, share, 0)
        common = jnp.concatenate([weights[0], nodes[0].astype(BF16), quarter.astype(BF16)])
        message = jnp.concatenate([binned, jnp.broadcast_to(common, (devices, common.shape[0]))], axis=1)
        message = lax.all_to_all(message, ALL, 0, 0, tiled=True).reshape(blocks, trees, -1)
        ends = (own * share, own * share + rows, own * share + 2 * rows)
        parts = [
            message[:, :, : ends[0]].reshape(blocks, trees, own, share).transpose(0, 2, 1, 3),
            message[:, :, ends[0] : ends[1]],
            message[:, :, ends[1] : ends[2]],
            message[:, :, ends[2] :],
        ]
        message = jnp.concatenate([p.reshape(blocks, -1, LANES) for p in parts], axis=1)[:, None]
        places = (
            lambda f, u: (0, f * chunks + u),
            lambda t, u: (0, (own + t) * chunks + u),
            lambda t, u: (0, (own + trees + t) * chunks + u),
            lambda u: (0, (own + 2 * trees) * chunks + u),
        )
    sizes = (blocks, chunks, trees, own)
    direct = split_features and NODES * trees * own == LANES
    here = lax.axis_index("rows") * lax.axis_size("feat") + lax.axis_index("feat")
    gains = score(message, places, sizes, direct, leaf)
    if direct:
        return pl.pallas_call(
            functools.partial(finish_kernel, blocks, trees, own),
            out_shape=(
                jax.ShapeDtypeStruct((1, NODES, trees * own), F32),
                jax.ShapeDtypeStruct((1, NODES), F32),
            ),
            in_specs=[SMEM, VMEM],
            out_specs=(pl.BlockSpec(), pl.BlockSpec()),
        )(here.reshape(1), lax.all_to_all(gains, ALL, 0, 0, tiled=True))
    outgoing = jnp.broadcast_to(gains.reshape(1, trees, NODES * own), (blocks, trees, NODES * own))
    scores = lax.all_to_all(outgoing.reshape(devices, NODES * own), ALL, 0, 0, tiled=True)
    scores = scores.reshape(blocks, trees, NODES, own)
    block = lax.dynamic_index_in_dim(scores, here, 0, keepdims=False)
    if split_features:
        split_gain = block.reshape(trees, NODES, trees, own // trees).transpose(1, 2, 0, 3)
    else:
        split_gain = block.transpose(1, 0, 2)
    return split_gain.reshape(1, NODES, trees * own), jnp.max(scores, axis=(0, 1, 3)).reshape(1, NODES)


def solution(mesh):
    shape = mesh.shape
    return jax.shard_map(
        functools.partial(local, blocks=shape["rows"] * shape["feat"], trees=shape["leaf"]),
        mesh=mesh,
        in_specs=(
            P(None, ("rows", "feat")),
            P(("rows", "feat")),
            P("leaf", ("rows", "feat")),
            P("leaf", ("rows", "feat")),
        ),
        out_specs=(P("leaf", None, ("rows", "feat")), P("leaf", None)),
        check_vma=False,
    )
```

```python
import functools
import math

import jax
import jax.numpy as jnp
from jax import lax
from jax.experimental import pallas as pl
from jax.experimental.pallas import tpu as pltpu
from jax.sharding import PartitionSpec as P

B = 128
C = 64
NODES = 2
STEP = 9.0 / B
LOWEST = math.ceil(-4 / STEP) + B // 2 - 1
HIGHEST = math.ceil(4 / STEP) + B // 2 - 1
LANES = 128
GROUP = 8
UNROLLED = 8
SPAN = 16
ALL = ("rows", "feat", "leaf")
BF16 = jnp.bfloat16
F32 = jnp.float32
VMEM = pl.BlockSpec(memory_space=pltpu.VMEM)
SMEM = pl.BlockSpec(memory_space=pltpu.SMEM)
HBM = pl.BlockSpec(memory_space=pltpu.HBM)


def bin_index(values):
    nearest = jnp.round(values * (1.0 / STEP))
    above = jnp.where(values > nearest * STEP, 1.0, 0.0)
    return jnp.clip(nearest + above + (B // 2 - 1), float(LOWEST), float(HIGHEST))


def iota(shape, axis):
    return lax.broadcasted_iota(jnp.int32, shape, axis).astype(F32)


def dot_lanes(a, b):
    return lax.dot_general(a, b, (((1,), (1,)), ((), ())), preferred_element_type=F32)


def sort_kernel(sizes, leaf_ref, here_ref, feature_ref, *refs):
    label_ref, weight_ref, node_ref, out_ref, slab, labels, weights, nodes, held, ordered, packed, sems = refs
    blocks, trees, own, rows, chunks, piece = sizes
    devices = blocks * trees
    copies = [
        pltpu.make_async_copy(source, to, sems.at[k])
        for k, (source, to) in enumerate(
            [
                (label_ref, labels),
                (weight_ref, weights),
                (node_ref, nodes),
                (feature_ref.at[:, leaf_ref[0]], slab),
            ]
        )
    ]
    for copy in copies:
        copy.start()
    copies[0].wait()
    label = labels[...].astype(F32)
    classes = iota((C, LANES), 0)
    hits, less = [], jnp.zeros((C, LANES), F32)
    for u in range(chunks):
        part = label[:, u * LANES : (u + 1) * LANES]
        hits.append(jnp.where(part == classes, 1.0, 0.0))
        less = less + jnp.where(part < classes, 1.0, 0.0)
    lower = jnp.where(iota((LANES, LANES), 0) < iota((LANES, LANES), 1), 1.0, 0.0)
    counter = jnp.concatenate([lower, jnp.ones((LANES, LANES), F32)], axis=1).astype(BF16)
    counts = jnp.dot(
        jnp.concatenate(hits + [less], axis=0).astype(BF16), counter, preferred_element_type=F32
    )
    first = counts[chunks * C :, LANES:]
    ranks = []
    for u in range(chunks):
        within = counts[u * C : (u + 1) * C]
        ranks.append(jnp.sum(hits[u] * (first + within[:, :LANES]), axis=0, keepdims=True))
        first = first + within[:, LANES:]
    spots = iota((rows, LANES), 0)
    order = jnp.concatenate([jnp.where(rank == spots, 1.0, 0.0).astype(BF16) for rank in ranks], axis=1)
    for copy in copies[1:]:
        copy.wait()
    held[devices * piece :, :] = jnp.concatenate(
        [weights[...].astype(F32), nodes[...].astype(F32), label, jnp.zeros((13, rows), F32)], axis=0
    ).astype(BF16)
    held[: devices * piece, :] = bin_index(slab[...].reshape(devices * piece, rows)).astype(BF16)
    sorted_rows = dot_lanes(held[...], order)
    for u in range(chunks):
        ordered[u] = sorted_rows[:, u * LANES : (u + 1) * LANES]
    deep = (piece + 3) * chunks
    for u in range(chunks):
        for k in range(piece):
            packed[pl.ds(k * chunks + u, devices, stride=deep), :] = ordered[u, pl.ds(k, devices, stride=piece), :]
    for k in range(3):
        tile = jnp.concatenate([ordered[u, devices * piece + k : devices * piece + k + 1, :] for u in range(chunks)], axis=0)
        for d in range(devices):
            at = d * deep + (piece + k) * chunks
            packed[at : at + chunks, :] = tile
    for d in range(devices):
        out_ref[d] = packed[d * deep : (d + 1) * deep, :].astype(BF16)


def score_kernel(places, sizes, direct, leaf_ref, here_ref, msg_ref, gain_ref, message, target, spread, total, whole, low, high):
    blocks, chunks, trees, own = sizes
    feature_at, weight_at, node_at, label_at = places
    groups = blocks // GROUP
    steps = groups * chunks
    depth = trees * NODES
    copies = LANES // own
    tiles = -(-(HIGHEST + 1 - LOWEST) // copies)
    first_bin = HIGHEST + 1 - tiles * copies
    share = total.shape[0] // steps
    message[...] = msg_ref[...].astype(F32)

    def row(block, place):
        return message[block, place[0], pl.ds(place[1], 1), :]

    def members(step):
        return [step // chunks * GROUP + g for g in range(GROUP)], step % chunks

    def set_target(step, base, to):
        held, u = members(step)
        for g, block in enumerate(held):
            label = row(block, label_at(u)) - base
            pairs = []
            for t in range(trees):
                weight, node = row(block, weight_at(t, u)), row(block, node_at(t, u))
                pairs += [jnp.where(node == n, weight, 0.0) for n in range(NODES)]
            pairs = jnp.concatenate(pairs, axis=0)
            for c in range(0, SPAN, 2):
                two = [jnp.where(label == c + more, pairs, 0.0) for more in range(2)]
                to[c * depth : (c + 2) * depth, g * LANES : (g + 1) * LANES] = jnp.concatenate(two, axis=0).astype(BF16)

    def prepare(step, carry):
        held, u = members(step)
        total[pl.ds(pl.multiple_of(step * share, 8), share), :] = jnp.zeros((share, total.shape[1]), F32)
        labels = jnp.concatenate([row(block, label_at(u)) for block in held], axis=0)
        least = jnp.min(labels)
        low[step] = least.astype(jnp.int32)
        high[step] = jnp.max(labels).astype(jnp.int32)
        set_target(step, least, target.at[step])
        for g, block in enumerate(held):
            tile = jnp.concatenate([row(block, feature_at(f, u)) for f in range(own)], axis=0)
            tile = jnp.concatenate([tile] * copies, axis=0)
            spread[step, g * LANES : (g + 1) * LANES, :] = tile.T.astype(BF16)
        return carry

    lax.fori_loop(0, steps, prepare, 0, unroll=4)
    bins = (first_bin + jnp.floor(iota((GROUP * LANES, LANES), 1) * (1.0 / own))).astype(BF16)
    one, zero = jnp.ones((), BF16), jnp.zeros((), BF16)

    def add(step, start, held):
        start = pl.multiple_of(start * depth, 8)
        for first in range(0, tiles, 2):
            last = min(first + 2, tiles)
            below = [
                jnp.where(spread[step] <= bins + float(tile * copies), one, zero)
                for tile in range(first, last)
            ]
            lanes = slice(first * LANES, last * LANES)
            total[pl.ds(start, SPAN * depth), lanes] += jnp.dot(
                held[...], jnp.concatenate(below, axis=1), preferred_element_type=F32
            )

    def more(step, carry):
        def one_pass(p, inner):
            base = low[step] + p * SPAN
            set_target(step, base.astype(F32), target.at[steps])
            add(step, base, target.at[steps])
            return inner

        return lax.fori_loop(1, (high[step] - low[step]) // SPAN + 1, one_pass, carry)

    for step in range(steps) if steps <= UNROLLED else ():
        add(step, low[step], target.at[step])
    if steps > UNROLLED:
        lax.fori_loop(0, steps, lambda step, carry: add(step, low[step], target.at[step]) or carry, 0)
    lax.fori_loop(0, steps, more, 0)

    def ratio(squares, sums):
        return squares / jnp.maximum(sums, 1.0)

    zeros = jnp.zeros((depth, LANES), F32)
    whole_sum, whole_square = zeros, zeros
    for c in range(C):
        part = jnp.broadcast_to(total[c * depth : (c + 1) * depth, tiles * LANES - 1 :], (depth, LANES))
        whole[c * depth : (c + 1) * depth, :] = part
        whole_sum, whole_square = whole_sum + part, whole_square + part * part
    whole_ratio = ratio(whole_square, whole_sum)
    best = jnp.full((depth, LANES), -jnp.inf, F32)
    for tile in range(tiles):
        left_sum, right_sum, left_square, right_square = zeros, zeros, zeros, zeros
        for c in range(C):
            left = total[c * depth : (c + 1) * depth, tile * LANES : (tile + 1) * LANES]
            right = whole[c * depth : (c + 1) * depth, :] - left
            left_sum, left_square = left_sum + left, left_square + left * left
            right_sum, right_square = right_sum + right, right_square + right * right
        gain = ratio(left_square, left_sum) + ratio(right_square, right_sum) - whole_ratio
        best = jnp.maximum(best, gain)
    shift = own
    while shift < LANES:
        best = jnp.maximum(best, pltpu.roll(best, shift, 1))
        shift *= 2
    if not direct:
        gain_ref[...] = best[:, :own]
        return
    piece = own // trees
    lane = lax.broadcasted_iota(jnp.int32, (depth, LANES), 1)
    sent = best
    for leaf in range(trees):
        moved = pltpu.roll(best, lax.rem((leaf_ref[0] - leaf) * piece + LANES, LANES), 1)
        sent = jnp.where(lane // own % trees == leaf, moved, sent)
    for t in range(trees):
        line = jnp.where(lane[:1] < trees * own, sent[t * NODES : t * NODES + 1], sent[t * NODES + 1 : t * NODES + 2])
        for block in range(blocks):
            gain_ref[block * trees + t] = line


def finish_kernel(blocks, trees, own, here_ref, msg_ref, gain_ref, best_ref):
    piece = own // trees
    half = trees * own
    lane = lax.broadcasted_iota(jnp.int32, (1, LANES), 1)
    mine = msg_ref[here_ref[0] * trees]
    for leaf in range(1, trees):
        mine = jnp.where(lane // piece % trees == leaf, msg_ref[here_ref[0] * trees + leaf], mine)
    top = msg_ref[0]
    for d in range(1, blocks * trees):
        top = jnp.maximum(top, msg_ref[d])
    for n in range(NODES):
        gain_ref[0, n : n + 1, :] = mine[:, n * half : (n + 1) * half]
        best_ref[:, n : n + 1] = jnp.max(top[:, n * half : (n + 1) * half], axis=1, keepdims=True)


def score(message, places, sizes, direct, leaf, here):
    blocks, chunks, trees, own = sizes
    depth = trees * NODES
    steps = blocks * chunks // GROUP
    columns = -(-(HIGHEST + 1 - LOWEST) * own // LANES) * LANES
    return pl.pallas_call(
        functools.partial(score_kernel, places, sizes, direct),
        out_shape=jax.ShapeDtypeStruct((blocks * trees, 1, LANES) if direct else (depth, own), F32),
        in_specs=[SMEM, SMEM, VMEM],
        out_specs=VMEM,
        scratch_shapes=[
            pltpu.VMEM(message.shape, F32),
            pltpu.VMEM((steps + 1, SPAN * depth, GROUP * LANES), BF16),
            pltpu.VMEM((steps, GROUP * LANES, LANES), BF16),
            pltpu.VMEM((-(-(C + SPAN) // steps) * steps * depth, columns), F32),
            pltpu.VMEM((C * depth, LANES), F32),
            pltpu.SMEM((steps,), jnp.int32),
            pltpu.SMEM((steps,), jnp.int32),
        ],
        compiler_params=pltpu.CompilerParams(vmem_limit_bytes=40 << 20),
    )(leaf, here, message)


def local(features, labels, weights, nodes, *, blocks, trees):
    feature_total, rows = features.shape
    own = feature_total // (blocks * trees)
    devices = blocks * trees
    leaf = lax.axis_index("leaf").reshape(1)
    here = (lax.axis_index("rows") * lax.axis_size("feat") + lax.axis_index("feat")).reshape(1)
    chunks = rows // LANES
    split_features = own % trees == 0
    if split_features:
        piece = own // trees
        deep = (piece + 3) * chunks
        held = devices * piece
        message = pl.pallas_call(
            functools.partial(sort_kernel, (blocks, trees, own, rows, chunks, piece)),
            out_shape=jax.ShapeDtypeStruct((devices, deep, LANES), BF16),
            in_specs=[
                SMEM,
                SMEM,
                HBM,
                HBM,
                HBM,
                HBM,
            ],
            out_specs=VMEM,
            scratch_shapes=[
                pltpu.VMEM((blocks, own, rows), F32),
                pltpu.VMEM((1, rows), jnp.int32),
                pltpu.VMEM((1, rows), BF16),
                pltpu.VMEM((1, rows), jnp.int32),
                pltpu.VMEM((held + 16, rows), BF16),
                pltpu.VMEM((chunks, held + 16, LANES), F32),
                pltpu.VMEM((devices * deep, LANES), F32),
                pltpu.SemaphoreType.DMA((4,)),
            ],
            compiler_params=pltpu.CompilerParams(vmem_limit_bytes=60 << 20),
        )(leaf, here, features.reshape(blocks, trees, own, rows), labels.reshape(1, rows), weights, nodes)
        message = lax.all_to_all(message, ALL, 0, 0, tiled=True)
        message = message.reshape(blocks, trees, deep, LANES)
        places = (
            lambda f, u: (f // piece, (f % piece) * chunks + u),
            lambda t, u: (t, piece * chunks + u),
            lambda t, u: (t, (piece + 1) * chunks + u),
            lambda u: (0, (piece + 2) * chunks + u),
        )
    else:
        share = rows // trees
        mine = lax.dynamic_slice_in_dim(features, leaf[0] * share, share, 1)
        binned = bin_index(mine).astype(BF16).reshape(devices, own * share)
        quarter = lax.dynamic_slice_in_dim(labels, leaf[0] * share, share, 0)
        common = jnp.concatenate([weights[0], nodes[0].astype(BF16), quarter.astype(BF16)])
        message = jnp.concatenate([binned, jnp.broadcast_to(common, (devices, common.shape[0]))], axis=1)
        message = lax.all_to_all(message, ALL, 0, 0, tiled=True).reshape(blocks, trees, -1)
        ends = (own * share, own * share + rows, own * share + 2 * rows)
        parts = [
            message[:, :, : ends[0]].reshape(blocks, trees, own, share).transpose(0, 2, 1, 3),
            message[:, :, ends[0] : ends[1]],
            message[:, :, ends[1] : ends[2]],
            message[:, :, ends[2] :],
        ]
        message = jnp.concatenate([p.reshape(blocks, -1, LANES) for p in parts], axis=1)[:, None]
        places = (
            lambda f, u: (0, f * chunks + u),
            lambda t, u: (0, (own + t) * chunks + u),
            lambda t, u: (0, (own + trees + t) * chunks + u),
            lambda u: (0, (own + 2 * trees) * chunks + u),
        )
    sizes = (blocks, chunks, trees, own)
    direct = split_features and NODES * trees * own == LANES
    gains = score(message, places, sizes, direct, leaf, here)
    if direct:
        return pl.pallas_call(
            functools.partial(finish_kernel, blocks, trees, own),
            out_shape=(
                jax.ShapeDtypeStruct((1, NODES, trees * own), F32),
                jax.ShapeDtypeStruct((1, NODES), F32),
            ),
            in_specs=[SMEM, VMEM],
            out_specs=(pl.BlockSpec(), pl.BlockSpec()),
        )(here, lax.all_to_all(gains, ALL, 0, 0, tiled=True))
    outgoing = jnp.broadcast_to(gains.reshape(1, trees, NODES * own), (blocks, trees, NODES * own))
    scores = lax.all_to_all(outgoing.reshape(devices, NODES * own), ALL, 0, 0, tiled=True)
    scores = scores.reshape(blocks, trees, NODES, own)
    block = lax.dynamic_index_in_dim(scores, here[0], 0, keepdims=False)
    if split_features:
        split_gain = block.reshape(trees, NODES, trees, own // trees).transpose(1, 2, 0, 3)
    else:
        split_gain = block.transpose(1, 0, 2)
    return split_gain.reshape(1, NODES, trees * own), jnp.max(scores, axis=(0, 1, 3)).reshape(1, NODES)


def solution(mesh):
    shape = mesh.shape
    return jax.shard_map(
        functools.partial(local, blocks=shape["rows"] * shape["feat"], trees=shape["leaf"]),
        mesh=mesh,
        in_specs=(
            P(None, ("rows", "feat")),
            P(("rows", "feat")),
            P("leaf", ("rows", "feat")),
            P("leaf", ("rows", "feat")),
        ),
        out_specs=(P("leaf", None, ("rows", "feat")), P("leaf", None)),
        check_vma=False,
    )
```

```python
import functools
import math

import jax
import jax.numpy as jnp
from jax import lax
from jax.experimental import pallas as pl
from jax.experimental.pallas import tpu as pltpu
from jax.sharding import PartitionSpec as P

B = 128
C = 64
NODES = 2
STEP = 9.0 / B
LOWEST = math.ceil(-4 / STEP) + B // 2 - 1
HIGHEST = math.ceil(4 / STEP) + B // 2 - 1
LANES = 128
GROUP = 8
UNROLLED = 8
SPAN = 16
ALL = ("rows", "feat", "leaf")
BF16 = jnp.bfloat16
F32 = jnp.float32
VMEM = pl.BlockSpec(memory_space=pltpu.VMEM)
SMEM = pl.BlockSpec(memory_space=pltpu.SMEM)
HBM = pl.BlockSpec(memory_space=pltpu.HBM)


def bin_index(values):
    nearest = jnp.round(values * (1.0 / STEP))
    above = jnp.where(values > nearest * STEP, 1.0, 0.0)
    return jnp.clip(nearest + above + (B // 2 - 1), float(LOWEST), float(HIGHEST))


def iota(shape, axis):
    return lax.broadcasted_iota(jnp.int32, shape, axis).astype(F32)


def dot_lanes(a, b):
    return lax.dot_general(a, b, (((1,), (1,)), ((), ())), preferred_element_type=F32)


def sort_kernel(sizes, leaf_ref, here_ref, feature_ref, *refs):
    label_ref, weight_ref, node_ref, out_ref, slab, labels, weights, nodes, held, ordered, packed, sems = refs
    blocks, trees, own, rows, chunks, piece = sizes
    devices = blocks * trees
    copies = [
        pltpu.make_async_copy(source, to, sems.at[k])
        for k, (source, to) in enumerate(
            [
                (label_ref, labels),
                (weight_ref, weights),
                (node_ref, nodes),
                (feature_ref.at[:, leaf_ref[0]], slab),
            ]
        )
    ]
    for copy in copies:
        copy.start()
    copies[0].wait()
    label = labels[...].astype(F32)
    classes = iota((C, LANES), 0)
    hits, less = [], jnp.zeros((C, LANES), F32)
    for u in range(chunks):
        part = label[:, u * LANES : (u + 1) * LANES]
        hits.append(jnp.where(part == classes, 1.0, 0.0))
        less = less + jnp.where(part < classes, 1.0, 0.0)
    lower = jnp.where(iota((LANES, LANES), 0) < iota((LANES, LANES), 1), 1.0, 0.0)
    counter = jnp.concatenate([lower, jnp.ones((LANES, LANES), F32)], axis=1).astype(BF16)
    counts = jnp.dot(
        jnp.concatenate(hits + [less], axis=0).astype(BF16), counter, preferred_element_type=F32
    )
    first = counts[chunks * C :, LANES:]
    ranks = []
    for u in range(chunks):
        within = counts[u * C : (u + 1) * C]
        ranks.append(jnp.sum(hits[u] * (first + within[:, :LANES]), axis=0, keepdims=True))
        first = first + within[:, LANES:]
    spots = iota((rows, LANES), 0)
    order = jnp.concatenate([jnp.where(rank == spots, 1.0, 0.0).astype(BF16) for rank in ranks], axis=1)
    for copy in copies[1:]:
        copy.wait()
    held[devices * piece :, :] = jnp.concatenate(
        [weights[...].astype(F32), nodes[...].astype(F32), label, jnp.zeros((13, rows), F32)], axis=0
    ).astype(BF16)
    held[: devices * piece, :] = bin_index(slab[...].reshape(devices * piece, rows)).astype(BF16)
    sorted_rows = dot_lanes(held[...], order)
    for u in range(chunks):
        ordered[u] = sorted_rows[:, u * LANES : (u + 1) * LANES]
    deep = (piece + 3) * chunks
    for u in range(chunks):
        for k in range(piece):
            packed[pl.ds(k * chunks + u, devices, stride=deep), :] = ordered[u, pl.ds(k, devices, stride=piece), :]
    for k in range(3):
        tile = jnp.concatenate([ordered[u, devices * piece + k : devices * piece + k + 1, :] for u in range(chunks)], axis=0)
        for d in range(devices):
            at = d * deep + (piece + k) * chunks
            packed[at : at + chunks, :] = tile
    for d in range(devices):
        out_ref[d] = packed[d * deep : (d + 1) * deep, :].astype(BF16)


def score_kernel(places, sizes, direct, leaf_ref, here_ref, msg_ref, gain_ref, message, target, spread, total, whole, low, high):
    blocks, chunks, trees, own = sizes
    feature_at, weight_at, node_at, label_at = places
    groups = blocks // GROUP
    steps = groups * chunks
    depth = trees * NODES
    copies = LANES // own
    tiles = -(-(HIGHEST + 1 - LOWEST) // copies)
    first_bin = HIGHEST + 1 - tiles * copies
    message[...] = msg_ref[...].astype(F32)
    total[: C * depth, :] = jnp.zeros((C * depth, total.shape[1]), F32)

    def row(block, place):
        return message[block, place[0], pl.ds(place[1], 1), :]

    def members(step):
        return [step // chunks * GROUP + g for g in range(GROUP)], step % chunks

    def set_target(block, u, lanes, base, to):
        label = row(block, label_at(u)) - base
        pairs = []
        for t in range(trees):
            weight, node = row(block, weight_at(t, u)), row(block, node_at(t, u))
            pairs += [jnp.where(node == n, weight, 0.0) for n in range(NODES)]
        pairs = jnp.concatenate(pairs, axis=0)
        for c in range(0, SPAN, 2):
            two = [jnp.where(label == c + more, pairs, 0.0) for more in range(2)]
            to[c * depth : (c + 2) * depth, lanes] = jnp.concatenate(two, axis=0).astype(BF16)

    def set_limits(step):
        held, u = members(step)
        labels = jnp.concatenate([row(block, label_at(u)) for block in held], axis=0)
        low[step] = jnp.min(labels).astype(jnp.int32)
        high[step] = jnp.max(labels).astype(jnp.int32)

    def prepare(step, g):
        held, u = members(step)
        lanes = slice(g * LANES, (g + 1) * LANES)
        set_target(held[g], u, lanes, low[step].astype(F32), target.at[step])
        tile = jnp.concatenate([row(held[g], feature_at(f, u)) for f in range(own)], axis=0)
        tile = jnp.concatenate([tile] * copies, axis=0)
        spread[step, lanes, :] = tile.T.astype(BF16)

    bins = (first_bin + jnp.floor(iota((GROUP * LANES, LANES), 1) * (1.0 / own))).astype(BF16)
    one, zero = jnp.ones((), BF16), jnp.zeros((), BF16)

    def add(step, start, held, beside=None):
        start = pl.multiple_of(start * depth, 8)
        for at, first in enumerate(range(0, tiles, 2)):
            last = min(first + 2, tiles)
            below = [
                jnp.minimum(jnp.maximum((bins + float(tile * copies + 1)) - spread[step], zero), one)
                for tile in range(first, last)
            ]
            lanes = slice(first * LANES, last * LANES)
            total[pl.ds(start, SPAN * depth), lanes] += jnp.dot(
                held[...], jnp.concatenate(below, axis=1), preferred_element_type=F32
            )
            if beside is not None:
                for g in range(at, GROUP, -(-tiles // 2)):
                    prepare(beside, g)

    def more(step, carry):
        def one_pass(p, inner):
            base = low[step] + p * SPAN
            held, u = members(step)
            for g in range(GROUP):
                lanes = slice(g * LANES, (g + 1) * LANES)
                set_target(held[g], u, lanes, base.astype(F32), target.at[steps])
            add(step, base, target.at[steps])
            return inner

        return lax.fori_loop(1, (high[step] - low[step]) // SPAN + 1, one_pass, carry)

    def window(step, carry):
        set_limits(step)
        for g in range(GROUP):
            prepare(step, g)
        add(step, low[step], target.at[step])
        return carry

    if steps <= UNROLLED:
        for step in range(steps):
            set_limits(step)
        for g in range(GROUP):
            prepare(0, g)
        for step in range(steps):
            add(step, low[step], target.at[step], step + 1 if step + 1 < steps else None)
    else:
        lax.fori_loop(0, steps, window, 0)
    lax.fori_loop(0, steps, more, 0)

    def ratio(squares, sums):
        return squares / jnp.maximum(sums, 1.0)

    zeros = jnp.zeros((depth, LANES), F32)
    whole_sum, whole_square = zeros, zeros
    for c in range(C):
        part = jnp.broadcast_to(total[c * depth : (c + 1) * depth, tiles * LANES - 1 :], (depth, LANES))
        whole[c * depth : (c + 1) * depth, :] = part
        whole_sum, whole_square = whole_sum + part, whole_square + part * part
    whole_ratio = ratio(whole_square, whole_sum)
    best = jnp.full((depth, LANES), -jnp.inf, F32)
    for tile in range(tiles):
        left_sum, right_sum, left_square, right_square = zeros, zeros, zeros, zeros
        for c in range(C):
            left = total[c * depth : (c + 1) * depth, tile * LANES : (tile + 1) * LANES]
            right = whole[c * depth : (c + 1) * depth, :] - left
            left_sum, left_square = left_sum + left, left_square + left * left
            right_sum, right_square = right_sum + right, right_square + right * right
        gain = ratio(left_square, left_sum) + ratio(right_square, right_sum) - whole_ratio
        best = jnp.maximum(best, gain)
    shift = own
    while shift < LANES:
        best = jnp.maximum(best, pltpu.roll(best, shift, 1))
        shift *= 2
    if not direct:
        gain_ref[...] = best[:, :own]
        return
    piece = own // trees
    lane = lax.broadcasted_iota(jnp.int32, (depth, LANES), 1)
    sent = best
    for leaf in range(trees):
        moved = pltpu.roll(best, lax.rem((leaf_ref[0] - leaf) * piece + LANES, LANES), 1)
        sent = jnp.where(lane // own % trees == leaf, moved, sent)
    for t in range(trees):
        line = jnp.where(lane[:1] < trees * own, sent[t * NODES : t * NODES + 1], sent[t * NODES + 1 : t * NODES + 2])
        for block in range(blocks):
            gain_ref[block * trees + t] = line


def finish_kernel(blocks, trees, own, here_ref, msg_ref, gain_ref, best_ref):
    piece = own // trees
    half = trees * own
    lane = lax.broadcasted_iota(jnp.int32, (1, LANES), 1)
    mine = msg_ref[here_ref[0] * trees]
    for leaf in range(1, trees):
        mine = jnp.where(lane // piece % trees == leaf, msg_ref[here_ref[0] * trees + leaf], mine)
    top = msg_ref[0]
    for d in range(1, blocks * trees):
        top = jnp.maximum(top, msg_ref[d])
    for n in range(NODES):
        gain_ref[0, n : n + 1, :] = mine[:, n * half : (n + 1) * half]
        best_ref[:, n : n + 1] = jnp.max(top[:, n * half : (n + 1) * half], axis=1, keepdims=True)


def score(message, places, sizes, direct, leaf, here):
    blocks, chunks, trees, own = sizes
    depth = trees * NODES
    steps = blocks * chunks // GROUP
    columns = -(-(HIGHEST + 1 - LOWEST) * own // LANES) * LANES
    return pl.pallas_call(
        functools.partial(score_kernel, places, sizes, direct),
        out_shape=jax.ShapeDtypeStruct((blocks * trees, 1, LANES) if direct else (depth, own), F32),
        in_specs=[SMEM, SMEM, VMEM],
        out_specs=VMEM,
        scratch_shapes=[
            pltpu.VMEM(message.shape, F32),
            pltpu.VMEM((steps + 1, SPAN * depth, GROUP * LANES), BF16),
            pltpu.VMEM((steps, GROUP * LANES, LANES), BF16),
            pltpu.VMEM(((C + SPAN) * depth, columns), F32),
            pltpu.VMEM((C * depth, LANES), F32),
            pltpu.SMEM((steps,), jnp.int32),
            pltpu.SMEM((steps,), jnp.int32),
        ],
        compiler_params=pltpu.CompilerParams(vmem_limit_bytes=40 << 20),
    )(leaf, here, message)


def local(features, labels, weights, nodes, *, blocks, trees):
    feature_total, rows = features.shape
    own = feature_total // (blocks * trees)
    devices = blocks * trees
    leaf = lax.axis_index("leaf").reshape(1)
    here = (lax.axis_index("rows") * lax.axis_size("feat") + lax.axis_index("feat")).reshape(1)
    chunks = rows // LANES
    split_features = own % trees == 0
    if split_features:
        piece = own // trees
        deep = (piece + 3) * chunks
        held = devices * piece
        message = pl.pallas_call(
            functools.partial(sort_kernel, (blocks, trees, own, rows, chunks, piece)),
            out_shape=jax.ShapeDtypeStruct((devices, deep, LANES), BF16),
            in_specs=[
                SMEM,
                SMEM,
                HBM,
                HBM,
                HBM,
                HBM,
            ],
            out_specs=VMEM,
            scratch_shapes=[
                pltpu.VMEM((blocks, own, rows), F32),
                pltpu.VMEM((1, rows), jnp.int32),
                pltpu.VMEM((1, rows), BF16),
                pltpu.VMEM((1, rows), jnp.int32),
                pltpu.VMEM((held + 16, rows), BF16),
                pltpu.VMEM((chunks, held + 16, LANES), F32),
                pltpu.VMEM((devices * deep, LANES), F32),
                pltpu.SemaphoreType.DMA((4,)),
            ],
            compiler_params=pltpu.CompilerParams(vmem_limit_bytes=60 << 20),
        )(leaf, here, features.reshape(blocks, trees, own, rows), labels.reshape(1, rows), weights, nodes)
        message = lax.all_to_all(message, ALL, 0, 0, tiled=True)
        message = message.reshape(blocks, trees, deep, LANES)
        places = (
            lambda f, u: (f // piece, (f % piece) * chunks + u),
            lambda t, u: (t, piece * chunks + u),
            lambda t, u: (t, (piece + 1) * chunks + u),
            lambda u: (0, (piece + 2) * chunks + u),
        )
    else:
        share = rows // trees
        mine = lax.dynamic_slice_in_dim(features, leaf[0] * share, share, 1)
        binned = bin_index(mine).astype(BF16).reshape(devices, own * share)
        quarter = lax.dynamic_slice_in_dim(labels, leaf[0] * share, share, 0)
        common = jnp.concatenate([weights[0], nodes[0].astype(BF16), quarter.astype(BF16)])
        message = jnp.concatenate([binned, jnp.broadcast_to(common, (devices, common.shape[0]))], axis=1)
        message = lax.all_to_all(message, ALL, 0, 0, tiled=True).reshape(blocks, trees, -1)
        ends = (own * share, own * share + rows, own * share + 2 * rows)
        parts = [
            message[:, :, : ends[0]].reshape(blocks, trees, own, share).transpose(0, 2, 1, 3),
            message[:, :, ends[0] : ends[1]],
            message[:, :, ends[1] : ends[2]],
            message[:, :, ends[2] :],
        ]
        message = jnp.concatenate([p.reshape(blocks, -1, LANES) for p in parts], axis=1)[:, None]
        places = (
            lambda f, u: (0, f * chunks + u),
            lambda t, u: (0, (own + t) * chunks + u),
            lambda t, u: (0, (own + trees + t) * chunks + u),
            lambda u: (0, (own + 2 * trees) * chunks + u),
        )
    sizes = (blocks, chunks, trees, own)
    direct = split_features and NODES * trees * own == LANES
    gains = score(message, places, sizes, direct, leaf, here)
    if direct:
        return pl.pallas_call(
            functools.partial(finish_kernel, blocks, trees, own),
            out_shape=(
                jax.ShapeDtypeStruct((1, NODES, trees * own), F32),
                jax.ShapeDtypeStruct((1, NODES), F32),
            ),
            in_specs=[SMEM, VMEM],
            out_specs=(pl.BlockSpec(), pl.BlockSpec()),
        )(here, lax.all_to_all(gains, ALL, 0, 0, tiled=True))
    outgoing = jnp.broadcast_to(gains.reshape(1, trees, NODES * own), (blocks, trees, NODES * own))
    scores = lax.all_to_all(outgoing.reshape(devices, NODES * own), ALL, 0, 0, tiled=True)
    scores = scores.reshape(blocks, trees, NODES, own)
    block = lax.dynamic_index_in_dim(scores, here[0], 0, keepdims=False)
    if split_features:
        split_gain = block.reshape(trees, NODES, trees, own // trees).transpose(1, 2, 0, 3)
    else:
        split_gain = block.transpose(1, 0, 2)
    return split_gain.reshape(1, NODES, trees * own), jnp.max(scores, axis=(0, 1, 3)).reshape(1, NODES)


def solution(mesh):
    shape = mesh.shape
    return jax.shard_map(
        functools.partial(local, blocks=shape["rows"] * shape["feat"], trees=shape["leaf"]),
        mesh=mesh,
        in_specs=(
            P(None, ("rows", "feat")),
            P(("rows", "feat")),
            P("leaf", ("rows", "feat")),
            P("leaf", ("rows", "feat")),
        ),
        out_specs=(P("leaf", None, ("rows", "feat")), P("leaf", None)),
        check_vma=False,
    )
```

```python
import functools
import math

import jax
import jax.numpy as jnp
from jax import lax
from jax.experimental import pallas as pl
from jax.experimental.pallas import tpu as pltpu
from jax.sharding import PartitionSpec as P

B = 128
C = 64
NODES = 2
STEP = 9.0 / B
LOWEST = math.ceil(-4 / STEP) + B // 2 - 1
HIGHEST = math.ceil(4 / STEP) + B // 2 - 1
LANES = 128
GROUP = 8
UNROLLED = 8
SPAN = 16
ALL = ("rows", "feat", "leaf")
BF16 = jnp.bfloat16
F32 = jnp.float32
VMEM = pl.BlockSpec(memory_space=pltpu.VMEM)
HBM = pl.BlockSpec(memory_space=pltpu.HBM)


def bin_index(values):
    nearest = jnp.round(values * (1.0 / STEP))
    above = jnp.where(values > nearest * STEP, 1.0, 0.0)
    return jnp.clip(nearest + above + (B // 2 - 1), float(LOWEST), float(HIGHEST))


def block_of_device():
    return lax.axis_index("rows") * lax.axis_size("feat") + lax.axis_index("feat")


def iota(shape, axis):
    return lax.broadcasted_iota(jnp.int32, shape, axis).astype(F32)


def dot_lanes(a, b):
    return lax.dot_general(a, b, (((1,), (1,)), ((), ())), preferred_element_type=F32)


def sort_kernel(sizes, feature_ref, *refs):
    label_ref, weight_ref, node_ref, out_ref, slab, labels, weights, nodes, held, ordered, packed, sems = refs
    blocks, trees, own, rows, chunks, piece = sizes
    devices = blocks * trees
    copies = [
        pltpu.make_async_copy(source, to, sems.at[k])
        for k, (source, to) in enumerate(
            [
                (label_ref, labels),
                (weight_ref, weights),
                (node_ref, nodes),
                (feature_ref.at[:, lax.axis_index("leaf")], slab),
            ]
        )
    ]
    for copy in copies:
        copy.start()
    copies[0].wait()
    label = labels[...].astype(F32)
    classes = iota((C, LANES), 0)
    hits, less = [], jnp.zeros((C, LANES), F32)
    for u in range(chunks):
        part = label[:, u * LANES : (u + 1) * LANES]
        hits.append(jnp.where(part == classes, 1.0, 0.0))
        less = less + jnp.where(part < classes, 1.0, 0.0)
    lower = jnp.where(iota((LANES, LANES), 0) < iota((LANES, LANES), 1), 1.0, 0.0)
    counter = jnp.concatenate([lower, jnp.ones((LANES, LANES), F32)], axis=1).astype(BF16)
    counts = jnp.dot(
        jnp.concatenate(hits + [less], axis=0).astype(BF16), counter, preferred_element_type=F32
    )
    first = counts[chunks * C :, LANES:]
    ranks = []
    for u in range(chunks):
        within = counts[u * C : (u + 1) * C]
        ranks.append(jnp.sum(hits[u] * (first + within[:, :LANES]), axis=0, keepdims=True))
        first = first + within[:, LANES:]
    spots = iota((rows, LANES), 0)
    order = jnp.concatenate([jnp.where(rank == spots, 1.0, 0.0).astype(BF16) for rank in ranks], axis=1)
    for copy in copies[1:]:
        copy.wait()
    held[devices * piece :, :] = jnp.concatenate(
        [weights[...].astype(F32), nodes[...].astype(F32), label, jnp.zeros((13, rows), F32)], axis=0
    ).astype(BF16)
    held[: devices * piece, :] = bin_index(slab[...].reshape(devices * piece, rows)).astype(BF16)
    sorted_rows = dot_lanes(held[...], order)
    for u in range(chunks):
        ordered[u] = sorted_rows[:, u * LANES : (u + 1) * LANES]
    deep = (piece + 3) * chunks
    for u in range(chunks):
        for k in range(piece):
            packed[pl.ds(k * chunks + u, devices, stride=deep), :] = ordered[u, pl.ds(k, devices, stride=piece), :]
    for k in range(3):
        tile = jnp.concatenate([ordered[u, devices * piece + k : devices * piece + k + 1, :] for u in range(chunks)], axis=0)
        for d in range(devices):
            at = d * deep + (piece + k) * chunks
            packed[at : at + chunks, :] = tile
    for d in range(devices):
        out_ref[d] = packed[d * deep : (d + 1) * deep, :].astype(BF16)


def score_kernel(places, sizes, direct, msg_ref, gain_ref, message, target, spread, total, whole, low, high):
    blocks, chunks, trees, own = sizes
    feature_at, weight_at, node_at, label_at = places
    groups = blocks // GROUP
    steps = groups * chunks
    depth = trees * NODES
    copies = LANES // own
    tiles = -(-(HIGHEST + 1 - LOWEST) // copies)
    first_bin = HIGHEST + 1 - tiles * copies
    firsts = range(0, tiles, 2)[::-1]
    message[...] = msg_ref[...].astype(F32)
    total[: C * depth, :] = jnp.zeros((C * depth, total.shape[1]), F32)

    def row(block, place):
        return message[block, place[0], pl.ds(place[1], 1), :]

    def members(step):
        return [step // chunks * GROUP + g for g in range(GROUP)], step % chunks

    def set_target(block, u, lanes, base, to):
        label = row(block, label_at(u)) - base
        pairs = []
        for t in range(trees):
            weight, node = row(block, weight_at(t, u)), row(block, node_at(t, u))
            pairs += [jnp.where(node == n, weight, 0.0) for n in range(NODES)]
        pairs = jnp.concatenate(pairs, axis=0)
        for c in range(0, SPAN, 2):
            two = [jnp.where(label == c + more, pairs, 0.0) for more in range(2)]
            to[c * depth : (c + 2) * depth, lanes] = jnp.concatenate(two, axis=0).astype(BF16)

    def set_limits(step):
        held, u = members(step)
        labels = jnp.concatenate([row(block, label_at(u)) for block in held], axis=0)
        low[step] = jnp.min(labels).astype(jnp.int32)
        high[step] = jnp.max(labels).astype(jnp.int32)

    def prepare(step, g):
        held, u = members(step)
        lanes = slice(g * LANES, (g + 1) * LANES)
        set_target(held[g], u, lanes, low[step].astype(F32), target.at[step])
        tile = jnp.concatenate([row(held[g], feature_at(f, u)) for f in range(own)], axis=0)
        tile = jnp.concatenate([tile] * copies, axis=0)
        spread[step, lanes, :] = tile.T.astype(BF16)

    bins = (first_bin + jnp.floor(iota((GROUP * LANES, LANES), 1) * (1.0 / own))).astype(BF16)
    one, zero = jnp.ones((), BF16), jnp.zeros((), BF16)

    def add(step, start, held, beside=None):
        start = pl.multiple_of(start * depth, 8)
        for at, first in enumerate(firsts):
            last = min(first + 2, tiles)
            below = [
                jnp.minimum(jnp.maximum((bins + float(tile * copies + 1)) - spread[step], zero), one)
                for tile in range(first, last)
            ]
            lanes = slice(first * LANES, last * LANES)
            total[pl.ds(start, SPAN * depth), lanes] += jnp.dot(
                held[...], jnp.concatenate(below, axis=1), preferred_element_type=F32
            )
            if beside is not None:
                beside(at)

    def more(step, carry):
        def one_pass(p, inner):
            base = low[step] + p * SPAN
            held, u = members(step)
            for g in range(GROUP):
                lanes = slice(g * LANES, (g + 1) * LANES)
                set_target(held[g], u, lanes, base.astype(F32), target.at[steps])
            add(step, base, target.at[steps])
            return inner

        return lax.fori_loop(1, (high[step] - low[step]) // SPAN + 1, one_pass, carry)

    def window(step, carry):
        set_limits(step)
        for g in range(GROUP):
            prepare(step, g)
        add(step, low[step], target.at[step])
        return carry

    def ratio(squares, sums):
        return squares / jnp.maximum(sums, 1.0)

    zeros = jnp.zeros((depth, LANES), F32)

    def set_whole():
        sums, squares = zeros, zeros
        for c in range(C):
            part = jnp.broadcast_to(total[c * depth : (c + 1) * depth, tiles * LANES - 1 :], (depth, LANES))
            whole[c * depth : (c + 1) * depth, :] = part
            sums, squares = sums + part, squares + part * part
        return ratio(squares, sums)

    def gain_of(tile, whole_ratio):
        left_sum, right_sum, left_square, right_square = zeros, zeros, zeros, zeros
        for c in range(C):
            left = total[c * depth : (c + 1) * depth, tile * LANES : (tile + 1) * LANES]
            right = whole[c * depth : (c + 1) * depth, :] - left
            left_sum, left_square = left_sum + left, left_square + left * left
            right_sum, right_square = right_sum + right, right_square + right * right
        return ratio(left_square, left_sum) + ratio(right_square, right_sum) - whole_ratio

    found = []
    if steps <= UNROLLED:
        for step in range(steps):
            set_limits(step)
        for g in range(GROUP):
            prepare(0, g)
        for step in range(steps - 1):

            def prepare_next(at, step=step):
                for g in range(at, GROUP, len(firsts)):
                    prepare(step + 1, g)

            add(step, low[step], target.at[step], prepare_next)
        lax.fori_loop(0, steps, more, 0)
        ratios = []

        def score_done(at):
            if at == 0:
                ratios.append(set_whole())
            else:
                first = firsts[at - 1]
                found.extend(gain_of(tile, ratios[0]) for tile in range(first, min(first + 2, tiles)))

        add(steps - 1, low[steps - 1], target.at[steps - 1], score_done)
        score_done(len(firsts))
    else:
        lax.fori_loop(0, steps, window, 0)
        lax.fori_loop(0, steps, more, 0)
        whole_ratio = set_whole()
        found.extend(gain_of(tile, whole_ratio) for tile in range(tiles))
    best = functools.reduce(jnp.maximum, found)
    shift = own
    while shift < LANES:
        best = jnp.maximum(best, pltpu.roll(best, shift, 1))
        shift *= 2
    if not direct:
        gain_ref[...] = best[:, :own]
        return
    piece = own // trees
    me = lax.axis_index("leaf")
    lane = lax.broadcasted_iota(jnp.int32, (depth, LANES), 1)
    sent = best
    for leaf in range(trees):
        moved = pltpu.roll(best, lax.rem((me - leaf) * piece + LANES, LANES), 1)
        sent = jnp.where(lane // own % trees == leaf, moved, sent)
    for t in range(trees):
        line = jnp.where(lane[:1] < trees * own, sent[t * NODES : t * NODES + 1], sent[t * NODES + 1 : t * NODES + 2])
        for block in range(blocks):
            gain_ref[block * trees + t] = line


def finish_kernel(blocks, trees, own, msg_ref, gain_ref, best_ref):
    here = block_of_device()
    piece = own // trees
    half = trees * own
    lane = lax.broadcasted_iota(jnp.int32, (1, LANES), 1)
    mine = msg_ref[here * trees]
    for leaf in range(1, trees):
        mine = jnp.where(lane // piece % trees == leaf, msg_ref[here * trees + leaf], mine)
    top = msg_ref[0]
    for d in range(1, blocks * trees):
        top = jnp.maximum(top, msg_ref[d])
    for n in range(NODES):
        gain_ref[0, n : n + 1, :] = mine[:, n * half : (n + 1) * half]
        best_ref[:, n : n + 1] = jnp.max(top[:, n * half : (n + 1) * half], axis=1, keepdims=True)


def score(message, places, sizes, direct):
    blocks, chunks, trees, own = sizes
    depth = trees * NODES
    steps = blocks * chunks // GROUP
    columns = -(-(HIGHEST + 1 - LOWEST) * own // LANES) * LANES
    return pl.pallas_call(
        functools.partial(score_kernel, places, sizes, direct),
        out_shape=jax.ShapeDtypeStruct((blocks * trees, 1, LANES) if direct else (depth, own), F32),
        in_specs=[VMEM],
        out_specs=VMEM,
        scratch_shapes=[
            pltpu.VMEM(message.shape, F32),
            pltpu.VMEM((steps + 1, SPAN * depth, GROUP * LANES), BF16),
            pltpu.VMEM((steps, GROUP * LANES, LANES), BF16),
            pltpu.VMEM(((C + SPAN) * depth, columns), F32),
            pltpu.VMEM((C * depth, LANES), F32),
            pltpu.SMEM((steps,), jnp.int32),
            pltpu.SMEM((steps,), jnp.int32),
        ],
        compiler_params=pltpu.CompilerParams(vmem_limit_bytes=40 << 20),
    )(message)


def local(features, labels, weights, nodes, *, blocks, trees):
    feature_total, rows = features.shape
    own = feature_total // (blocks * trees)
    devices = blocks * trees
    chunks = rows // LANES
    split_features = own % trees == 0
    if split_features:
        piece = own // trees
        deep = (piece + 3) * chunks
        held = devices * piece
        message = pl.pallas_call(
            functools.partial(sort_kernel, (blocks, trees, own, rows, chunks, piece)),
            out_shape=jax.ShapeDtypeStruct((devices, deep, LANES), BF16),
            in_specs=[
                HBM,
                HBM,
                HBM,
                HBM,
            ],
            out_specs=VMEM,
            scratch_shapes=[
                pltpu.VMEM((blocks, own, rows), F32),
                pltpu.VMEM((1, rows), jnp.int32),
                pltpu.VMEM((1, rows), BF16),
                pltpu.VMEM((1, rows), jnp.int32),
                pltpu.VMEM((held + 16, rows), BF16),
                pltpu.VMEM((chunks, held + 16, LANES), F32),
                pltpu.VMEM((devices * deep, LANES), F32),
                pltpu.SemaphoreType.DMA((4,)),
            ],
            compiler_params=pltpu.CompilerParams(vmem_limit_bytes=60 << 20),
        )(features.reshape(blocks, trees, own, rows), labels.reshape(1, rows), weights, nodes)
        message = lax.all_to_all(message, ALL, 0, 0, tiled=True)
        message = message.reshape(blocks, trees, deep, LANES)
        places = (
            lambda f, u: (f // piece, (f % piece) * chunks + u),
            lambda t, u: (t, piece * chunks + u),
            lambda t, u: (t, (piece + 1) * chunks + u),
            lambda u: (0, (piece + 2) * chunks + u),
        )
    else:
        share = rows // trees
        mine = lax.dynamic_slice_in_dim(features, lax.axis_index("leaf") * share, share, 1)
        binned = bin_index(mine).astype(BF16).reshape(devices, own * share)
        quarter = lax.dynamic_slice_in_dim(labels, lax.axis_index("leaf") * share, share, 0)
        common = jnp.concatenate([weights[0], nodes[0].astype(BF16), quarter.astype(BF16)])
        message = jnp.concatenate([binned, jnp.broadcast_to(common, (devices, common.shape[0]))], axis=1)
        message = lax.all_to_all(message, ALL, 0, 0, tiled=True).reshape(blocks, trees, -1)
        ends = (own * share, own * share + rows, own * share + 2 * rows)
        parts = [
            message[:, :, : ends[0]].reshape(blocks, trees, own, share).transpose(0, 2, 1, 3),
            message[:, :, ends[0] : ends[1]],
            message[:, :, ends[1] : ends[2]],
            message[:, :, ends[2] :],
        ]
        message = jnp.concatenate([p.reshape(blocks, -1, LANES) for p in parts], axis=1)[:, None]
        places = (
            lambda f, u: (0, f * chunks + u),
            lambda t, u: (0, (own + t) * chunks + u),
            lambda t, u: (0, (own + trees + t) * chunks + u),
            lambda u: (0, (own + 2 * trees) * chunks + u),
        )
    sizes = (blocks, chunks, trees, own)
    direct = split_features and NODES * trees * own == LANES
    gains = score(message, places, sizes, direct)
    if direct:
        return pl.pallas_call(
            functools.partial(finish_kernel, blocks, trees, own),
            out_shape=(
                jax.ShapeDtypeStruct((1, NODES, trees * own), F32),
                jax.ShapeDtypeStruct((1, NODES), F32),
            ),
            in_specs=[VMEM],
            out_specs=(pl.BlockSpec(), pl.BlockSpec()),
        )(lax.all_to_all(gains, ALL, 0, 0, tiled=True))
    outgoing = jnp.broadcast_to(gains.reshape(1, trees, NODES * own), (blocks, trees, NODES * own))
    scores = lax.all_to_all(outgoing.reshape(devices, NODES * own), ALL, 0, 0, tiled=True)
    scores = scores.reshape(blocks, trees, NODES, own)
    block = lax.dynamic_index_in_dim(scores, block_of_device(), 0, keepdims=False)
    if split_features:
        split_gain = block.reshape(trees, NODES, trees, own // trees).transpose(1, 2, 0, 3)
    else:
        split_gain = block.transpose(1, 0, 2)
    return split_gain.reshape(1, NODES, trees * own), jnp.max(scores, axis=(0, 1, 3)).reshape(1, NODES)


def solution(mesh):
    shape = mesh.shape
    return jax.shard_map(
        functools.partial(local, blocks=shape["rows"] * shape["feat"], trees=shape["leaf"]),
        mesh=mesh,
        in_specs=(
            P(None, ("rows", "feat")),
            P(("rows", "feat")),
            P("leaf", ("rows", "feat")),
            P("leaf", ("rows", "feat")),
        ),
        out_specs=(P("leaf", None, ("rows", "feat")), P("leaf", None)),
        check_vma=False,
    )
```

```python
import functools
import math

import jax
import jax.numpy as jnp
from jax import lax
from jax.experimental import pallas as pl
from jax.experimental.pallas import tpu as pltpu
from jax.sharding import PartitionSpec as P

B = 128
C = 64
NODES = 2
STEP = 9.0 / B
LOWEST = math.ceil(-4 / STEP) + B // 2 - 1
HIGHEST = math.ceil(4 / STEP) + B // 2 - 1
LANES = 128
GROUP = 8
UNROLLED = 8
SPAN = 16
ALL = ("rows", "feat", "leaf")
BF16 = jnp.bfloat16
F32 = jnp.float32
VMEM = pl.BlockSpec(memory_space=pltpu.VMEM)
HBM = pl.BlockSpec(memory_space=pltpu.HBM)


def bin_index(values):
    nearest = jnp.round(values * (1.0 / STEP))
    above = jnp.where(values > nearest * STEP, 1.0, 0.0)
    return jnp.clip(nearest + above + (B // 2 - 1), float(LOWEST), float(HIGHEST))


def block_of_device():
    return lax.axis_index("rows") * lax.axis_size("feat") + lax.axis_index("feat")


def iota(shape, axis):
    return lax.broadcasted_iota(jnp.int32, shape, axis).astype(F32)


def dot_lanes(a, b):
    return lax.dot_general(a, b, (((1,), (1,)), ((), ())), preferred_element_type=F32)


def sort_kernel(sizes, feature_ref, *refs):
    label_ref, weight_ref, node_ref, out_ref, slab, labels, weights, nodes, held, ordered, packed, sems = refs
    blocks, trees, own, rows, chunks, piece = sizes
    devices = blocks * trees
    copies = [
        pltpu.make_async_copy(source, to, sems.at[k])
        for k, (source, to) in enumerate(
            [
                (label_ref, labels),
                (weight_ref, weights),
                (node_ref, nodes),
                (feature_ref.at[:, lax.axis_index("leaf")], slab),
            ]
        )
    ]
    for copy in copies:
        copy.start()
    copies[0].wait()
    label = labels[...].astype(F32)
    classes = iota((C, LANES), 0)
    hits, less = [], jnp.zeros((C, LANES), F32)
    for u in range(chunks):
        part = label[:, u * LANES : (u + 1) * LANES]
        hits.append(jnp.where(part == classes, 1.0, 0.0))
        less = less + jnp.where(part < classes, 1.0, 0.0)
    lower = jnp.where(iota((LANES, LANES), 0) < iota((LANES, LANES), 1), 1.0, 0.0)
    counter = jnp.concatenate([lower, jnp.ones((LANES, LANES), F32)], axis=1).astype(BF16)
    counts = jnp.dot(
        jnp.concatenate(hits + [less], axis=0).astype(BF16), counter, preferred_element_type=F32
    )
    first = counts[chunks * C :, LANES:]
    ranks = []
    for u in range(chunks):
        within = counts[u * C : (u + 1) * C]
        ranks.append(jnp.sum(hits[u] * (first + within[:, :LANES]), axis=0, keepdims=True))
        first = first + within[:, LANES:]
    spots = iota((rows, LANES), 0)
    order = jnp.concatenate([jnp.where(rank == spots, 1.0, 0.0).astype(BF16) for rank in ranks], axis=1)
    for copy in copies[1:]:
        copy.wait()
    held[devices * piece :, :] = jnp.concatenate(
        [weights[...].astype(F32), nodes[...].astype(F32), label, jnp.zeros((13, rows), F32)], axis=0
    ).astype(BF16)
    held[: devices * piece, :] = bin_index(slab[...].reshape(devices * piece, rows)).astype(BF16)
    sorted_rows = dot_lanes(held[...], order)
    for u in range(chunks):
        ordered[u] = sorted_rows[:, u * LANES : (u + 1) * LANES]
    deep = (piece + 3) * chunks
    for u in range(chunks):
        for k in range(piece):
            packed[pl.ds(k * chunks + u, devices, stride=deep), :] = ordered[u, pl.ds(k, devices, stride=piece), :]
    for k in range(3):
        tile = jnp.concatenate([ordered[u, devices * piece + k : devices * piece + k + 1, :] for u in range(chunks)], axis=0)
        for d in range(devices):
            at = d * deep + (piece + k) * chunks
            packed[at : at + chunks, :] = tile
    for d in range(devices):
        out_ref[d] = packed[d * deep : (d + 1) * deep, :].astype(BF16)


def score_kernel(places, sizes, direct, msg_ref, gain_ref, message, target, spread, total, whole, low, high):
    blocks, chunks, trees, own = sizes
    feature_at, weight_at, node_at, label_at = places
    groups = blocks // GROUP
    steps = groups * chunks
    depth = trees * NODES
    copies = LANES // own
    tiles = -(-(HIGHEST + 1 - LOWEST) // copies)
    first_bin = HIGHEST + 1 - tiles * copies
    firsts = range(0, tiles, 2)[::-1]
    message[...] = msg_ref[...].astype(F32)
    total[: C * depth, :] = jnp.zeros((C * depth, total.shape[1]), F32)

    def row(block, place):
        return message[block, place[0], pl.ds(place[1], 1), :]

    def members(step):
        return [step // chunks * GROUP + g for g in range(GROUP)], step % chunks

    def set_target(block, u, lanes, base, to):
        label = row(block, label_at(u)) - base
        pairs = []
        for t in range(trees):
            weight, node = row(block, weight_at(t, u)), row(block, node_at(t, u))
            pairs += [jnp.where(node == n, weight, 0.0) for n in range(NODES)]
        pairs = jnp.concatenate(pairs, axis=0)
        for c in range(0, SPAN, 2):
            two = [jnp.where(label == c + more, pairs, 0.0) for more in range(2)]
            to[c * depth : (c + 2) * depth, lanes] = jnp.concatenate(two, axis=0).astype(BF16)

    def set_limits(step):
        held, u = members(step)
        labels = jnp.concatenate([row(block, label_at(u)) for block in held], axis=0)
        low[step] = jnp.min(labels).astype(jnp.int32)
        high[step] = jnp.max(labels).astype(jnp.int32)

    def prepare(step, g):
        held, u = members(step)
        lanes = slice(g * LANES, (g + 1) * LANES)
        set_target(held[g], u, lanes, low[step].astype(F32), target.at[step])
        tile = jnp.concatenate([row(held[g], feature_at(f, u)) for f in range(own)], axis=0)
        tile = jnp.concatenate([tile] * copies, axis=0)
        spread[step, lanes, :] = tile.T.astype(BF16)

    bins = (first_bin + jnp.floor(iota((GROUP * LANES, LANES), 1) * (1.0 / own))).astype(BF16)
    one, zero = jnp.ones((), BF16), jnp.zeros((), BF16)

    def add(step, start, held, beside=None):
        start = pl.multiple_of(start * depth, 8)
        for at, first in enumerate(firsts):
            last = min(first + 2, tiles)
            below = [
                jnp.minimum(jnp.maximum((bins + float(tile * copies + 1)) - spread[step], zero), one)
                for tile in range(first, last)
            ]
            lanes = slice(first * LANES, last * LANES)
            total[pl.ds(start, SPAN * depth), lanes] += jnp.dot(
                held[...], jnp.concatenate(below, axis=1), preferred_element_type=F32
            )
            if beside is not None:
                beside(at)

    def more(step, carry):
        def one_pass(p, inner):
            base = low[step] + p * SPAN
            held, u = members(step)
            for g in range(GROUP):
                lanes = slice(g * LANES, (g + 1) * LANES)
                set_target(held[g], u, lanes, base.astype(F32), target.at[steps])
            add(step, base, target.at[steps])
            return inner

        return lax.fori_loop(1, (high[step] - low[step]) // SPAN + 1, one_pass, carry)

    def window(step, carry):
        set_limits(step)
        for g in range(GROUP):
            prepare(step, g)
        add(step, low[step], target.at[step])
        return carry

    def ratio(squares, sums):
        return squares / jnp.maximum(sums, 1.0)

    zeros = jnp.zeros((depth, LANES), F32)

    def set_whole():
        sums, squares = zeros, zeros
        for c in range(C):
            part = jnp.broadcast_to(total[c * depth : (c + 1) * depth, tiles * LANES - 1 :], (depth, LANES))
            whole[c * depth : (c + 1) * depth, :] = part
            sums, squares = sums + part, squares + part * part
        return ratio(squares, sums)

    def gain_of(tile, whole_ratio):
        left_sum, right_sum, left_square, right_square = zeros, zeros, zeros, zeros
        for c in range(C):
            left = total[c * depth : (c + 1) * depth, tile * LANES : (tile + 1) * LANES]
            right = whole[c * depth : (c + 1) * depth, :] - left
            left_sum, left_square = left_sum + left, left_square + left * left
            right_sum, right_square = right_sum + right, right_square + right * right
        return ratio(left_square, left_sum) + ratio(right_square, right_sum) - whole_ratio

    found = []
    if steps <= UNROLLED:
        for step in range(steps):
            set_limits(step)
        for g in range(GROUP):
            prepare(0, g)
        for step in range(steps - 1):

            def prepare_next(at, step=step):
                for g in range(at, GROUP, len(firsts)):
                    prepare(step + 1, g)

            add(step, low[step], target.at[step], prepare_next)
        lax.fori_loop(0, steps, more, 0)
        ratios = []

        def score_done(at):
            if at == 0:
                ratios.append(set_whole())
            else:
                first = firsts[at - 1]
                found.extend(gain_of(tile, ratios[0]) for tile in range(first, min(first + 2, tiles)))

        add(steps - 1, low[steps - 1], target.at[steps - 1], score_done)
        score_done(len(firsts))
    else:
        lax.fori_loop(0, steps, window, 0)
        lax.fori_loop(0, steps, more, 0)
        whole_ratio = set_whole()
        found.extend(gain_of(tile, whole_ratio) for tile in range(tiles))
    best = functools.reduce(jnp.maximum, found)
    shift = own
    while shift < LANES:
        best = jnp.maximum(best, pltpu.roll(best, shift, 1))
        shift *= 2
    if not direct:
        gain_ref[...] = best[:, :own]
        return
    piece = own // trees
    me = lax.axis_index("leaf")
    lane = lax.broadcasted_iota(jnp.int32, (depth, LANES), 1)
    sent = best
    for leaf in range(trees):
        moved = pltpu.roll(best, lax.rem((me - leaf) * piece + LANES, LANES), 1)
        sent = jnp.where(lane // own % trees == leaf, moved, sent)
    for t in range(trees):
        line = jnp.where(lane[:1] < trees * own, sent[t * NODES : t * NODES + 1], sent[t * NODES + 1 : t * NODES + 2])
        for block in range(blocks):
            gain_ref[block * trees + t] = line


def finish_kernel(blocks, trees, own, msg_ref, gain_ref, best_ref):
    here = block_of_device()
    piece = own // trees
    half = trees * own
    lane = lax.broadcasted_iota(jnp.int32, (1, LANES), 1)
    mine = msg_ref[here * trees]
    for leaf in range(1, trees):
        mine = jnp.where(lane // piece % trees == leaf, msg_ref[here * trees + leaf], mine)
    chains = [
        functools.reduce(jnp.maximum, [msg_ref[block * trees + leaf] for block in range(blocks)]) for leaf in range(trees)
    ]
    top = functools.reduce(jnp.maximum, chains)
    for n in range(NODES):
        gain_ref[0, n : n + 1, :] = mine[:, n * half : (n + 1) * half]
        best_ref[:, n : n + 1] = jnp.max(top[:, n * half : (n + 1) * half], axis=1, keepdims=True)


def score(message, places, sizes, direct):
    blocks, chunks, trees, own = sizes
    depth = trees * NODES
    steps = blocks * chunks // GROUP
    columns = -(-(HIGHEST + 1 - LOWEST) * own // LANES) * LANES
    return pl.pallas_call(
        functools.partial(score_kernel, places, sizes, direct),
        out_shape=jax.ShapeDtypeStruct((blocks * trees, 1, LANES) if direct else (depth, own), F32),
        in_specs=[VMEM],
        out_specs=VMEM,
        scratch_shapes=[
            pltpu.VMEM(message.shape, F32),
            pltpu.VMEM((steps + 1, SPAN * depth, GROUP * LANES), BF16),
            pltpu.VMEM((steps, GROUP * LANES, LANES), BF16),
            pltpu.VMEM(((C + SPAN) * depth, columns), F32),
            pltpu.VMEM((C * depth, LANES), F32),
            pltpu.SMEM((steps,), jnp.int32),
            pltpu.SMEM((steps,), jnp.int32),
        ],
        compiler_params=pltpu.CompilerParams(vmem_limit_bytes=40 << 20),
    )(message)


def local(features, labels, weights, nodes, *, blocks, trees):
    feature_total, rows = features.shape
    own = feature_total // (blocks * trees)
    devices = blocks * trees
    chunks = rows // LANES
    split_features = own % trees == 0
    if split_features:
        piece = own // trees
        deep = (piece + 3) * chunks
        held = devices * piece
        message = pl.pallas_call(
            functools.partial(sort_kernel, (blocks, trees, own, rows, chunks, piece)),
            out_shape=jax.ShapeDtypeStruct((devices, deep, LANES), BF16),
            in_specs=[
                HBM,
                HBM,
                HBM,
                HBM,
            ],
            out_specs=VMEM,
            scratch_shapes=[
                pltpu.VMEM((blocks, own, rows), F32),
                pltpu.VMEM((1, rows), jnp.int32),
                pltpu.VMEM((1, rows), BF16),
                pltpu.VMEM((1, rows), jnp.int32),
                pltpu.VMEM((held + 16, rows), BF16),
                pltpu.VMEM((chunks, held + 16, LANES), F32),
                pltpu.VMEM(((devices + 1) * deep, LANES), F32),
                pltpu.SemaphoreType.DMA((4,)),
            ],
            compiler_params=pltpu.CompilerParams(vmem_limit_bytes=60 << 20),
        )(features.reshape(blocks, trees, own, rows), labels.reshape(1, rows), weights, nodes)
        message = lax.all_to_all(message, ALL, 0, 0, tiled=True)
        message = message.reshape(blocks, trees, deep, LANES)
        places = (
            lambda f, u: (f // piece, (f % piece) * chunks + u),
            lambda t, u: (t, piece * chunks + u),
            lambda t, u: (t, (piece + 1) * chunks + u),
            lambda u: (0, (piece + 2) * chunks + u),
        )
    else:
        share = rows // trees
        mine = lax.dynamic_slice_in_dim(features, lax.axis_index("leaf") * share, share, 1)
        binned = bin_index(mine).astype(BF16).reshape(devices, own * share)
        quarter = lax.dynamic_slice_in_dim(labels, lax.axis_index("leaf") * share, share, 0)
        common = jnp.concatenate([weights[0], nodes[0].astype(BF16), quarter.astype(BF16)])
        message = jnp.concatenate([binned, jnp.broadcast_to(common, (devices, common.shape[0]))], axis=1)
        message = lax.all_to_all(message, ALL, 0, 0, tiled=True).reshape(blocks, trees, -1)
        ends = (own * share, own * share + rows, own * share + 2 * rows)
        parts = [
            message[:, :, : ends[0]].reshape(blocks, trees, own, share).transpose(0, 2, 1, 3),
            message[:, :, ends[0] : ends[1]],
            message[:, :, ends[1] : ends[2]],
            message[:, :, ends[2] :],
        ]
        message = jnp.concatenate([p.reshape(blocks, -1, LANES) for p in parts], axis=1)[:, None]
        places = (
            lambda f, u: (0, f * chunks + u),
            lambda t, u: (0, (own + t) * chunks + u),
            lambda t, u: (0, (own + trees + t) * chunks + u),
            lambda u: (0, (own + 2 * trees) * chunks + u),
        )
    sizes = (blocks, chunks, trees, own)
    direct = split_features and NODES * trees * own == LANES
    gains = score(message, places, sizes, direct)
    if direct:
        return pl.pallas_call(
            functools.partial(finish_kernel, blocks, trees, own),
            out_shape=(
                jax.ShapeDtypeStruct((1, NODES, trees * own), F32),
                jax.ShapeDtypeStruct((1, NODES), F32),
            ),
            in_specs=[VMEM],
            out_specs=(pl.BlockSpec(), pl.BlockSpec()),
        )(lax.all_to_all(gains, ALL, 0, 0, tiled=True))
    outgoing = jnp.broadcast_to(gains.reshape(1, trees, NODES * own), (blocks, trees, NODES * own))
    scores = lax.all_to_all(outgoing.reshape(devices, NODES * own), ALL, 0, 0, tiled=True)
    scores = scores.reshape(blocks, trees, NODES, own)
    block = lax.dynamic_index_in_dim(scores, block_of_device(), 0, keepdims=False)
    if split_features:
        split_gain = block.reshape(trees, NODES, trees, own // trees).transpose(1, 2, 0, 3)
    else:
        split_gain = block.transpose(1, 0, 2)
    return split_gain.reshape(1, NODES, trees * own), jnp.max(scores, axis=(0, 1, 3)).reshape(1, NODES)


def solution(mesh):
    shape = mesh.shape
    return jax.shard_map(
        functools.partial(local, blocks=shape["rows"] * shape["feat"], trees=shape["leaf"]),
        mesh=mesh,
        in_specs=(
            P(None, ("rows", "feat")),
            P(("rows", "feat")),
            P("leaf", ("rows", "feat")),
            P("leaf", ("rows", "feat")),
        ),
        out_specs=(P("leaf", None, ("rows", "feat")), P("leaf", None)),
        check_vma=False,
    )
```

```python
import functools
import math

import jax
import jax.numpy as jnp
from jax import lax
from jax.experimental import pallas as pl
from jax.experimental.pallas import tpu as pltpu
from jax.sharding import PartitionSpec as P

B = 128
C = 64
NODES = 2
STEP = 9.0 / B
LOWEST = math.ceil(-4 / STEP) + B // 2 - 1
HIGHEST = math.ceil(4 / STEP) + B // 2 - 1
LANES = 128
GROUP = 8
UNROLLED = 8
SPAN = 16
ALL = ("rows", "feat", "leaf")
BF16 = jnp.bfloat16
F32 = jnp.float32
VMEM = pl.BlockSpec(memory_space=pltpu.VMEM)
HBM = pl.BlockSpec(memory_space=pltpu.HBM)


def bin_index(values):
    nearest = jnp.round(values * (1.0 / STEP))
    above = jnp.where(values > nearest * STEP, 1.0, 0.0)
    return jnp.clip(nearest + above + (B // 2 - 1), float(LOWEST), float(HIGHEST))


def block_of_device():
    return lax.axis_index("rows") * lax.axis_size("feat") + lax.axis_index("feat")


def iota(shape, axis):
    return lax.broadcasted_iota(jnp.int32, shape, axis).astype(F32)


def dot_lanes(a, b):
    return lax.dot_general(a, b, (((1,), (1,)), ((), ())), preferred_element_type=F32)


def sort_kernel(sizes, feature_ref, *refs):
    label_ref, weight_ref, node_ref, out_ref, slab, labels, weights, nodes, held, ordered, packed, sems = refs
    blocks, trees, own, rows, chunks, piece = sizes
    devices = blocks * trees
    copies = [
        pltpu.make_async_copy(source, to, sems.at[k])
        for k, (source, to) in enumerate(
            [
                (label_ref, labels),
                (weight_ref, weights),
                (node_ref, nodes),
                (feature_ref.at[:, lax.axis_index("leaf")], slab),
            ]
        )
    ]
    for copy in copies:
        copy.start()
    copies[0].wait()
    label = labels[...].astype(F32)
    classes = iota((C, LANES), 0)
    hits, less = [], jnp.zeros((C, LANES), F32)
    for u in range(chunks):
        part = label[:, u * LANES : (u + 1) * LANES]
        hits.append(jnp.where(part == classes, 1.0, 0.0))
        less = less + jnp.where(part < classes, 1.0, 0.0)
    lower = jnp.where(iota((LANES, LANES), 0) < iota((LANES, LANES), 1), 1.0, 0.0)
    counter = jnp.concatenate([lower, jnp.ones((LANES, LANES), F32)], axis=1).astype(BF16)
    counts = jnp.dot(
        jnp.concatenate(hits + [less], axis=0).astype(BF16), counter, preferred_element_type=F32
    )
    first = counts[chunks * C :, LANES:]
    ranks = []
    for u in range(chunks):
        within = counts[u * C : (u + 1) * C]
        ranks.append(jnp.sum(hits[u] * (first + within[:, :LANES]), axis=0, keepdims=True))
        first = first + within[:, LANES:]
    spots = iota((rows, LANES), 0)
    order = jnp.concatenate([jnp.where(rank == spots, 1.0, 0.0).astype(BF16) for rank in ranks], axis=1)
    for copy in copies[1:]:
        copy.wait()
    held[devices * piece :, :] = jnp.concatenate(
        [weights[...].astype(F32), nodes[...].astype(F32), label, jnp.zeros((13, rows), F32)], axis=0
    ).astype(BF16)
    held[: devices * piece, :] = bin_index(slab[...].reshape(devices * piece, rows)).astype(BF16)
    sorted_rows = dot_lanes(held[...], order)
    for u in range(chunks):
        ordered[u] = sorted_rows[:, u * LANES : (u + 1) * LANES]
    deep = (piece + 3) * chunks
    for u in range(chunks):
        for k in range(piece):
            packed[pl.ds(k * chunks + u, devices, stride=deep), :] = ordered[u, pl.ds(k, devices, stride=piece), :]
    for k in range(3):
        tile = jnp.concatenate([ordered[u, devices * piece + k : devices * piece + k + 1, :] for u in range(chunks)], axis=0)
        for d in range(devices):
            at = d * deep + (piece + k) * chunks
            packed[at : at + chunks, :] = tile
    for d in range(devices):
        out_ref[d] = packed[d * deep : (d + 1) * deep, :].astype(BF16)


def score_kernel(places, sizes, direct, msg_ref, gain_ref, message, target, spread, total, whole, low, high):
    blocks, chunks, trees, own = sizes
    feature_at, weight_at, node_at, label_at = places
    groups = blocks // GROUP
    steps = groups * chunks
    depth = trees * NODES
    copies = LANES // own
    tiles = -(-(HIGHEST + 1 - LOWEST) // copies)
    first_bin = HIGHEST + 1 - tiles * copies
    firsts = range(0, tiles, 2)[::-1]
    message[...] = msg_ref[...].astype(F32)
    total[: C * depth, :] = jnp.zeros((C * depth, total.shape[1]), F32)

    def row(block, place):
        return message[block, place[0], pl.ds(place[1], 1), :]

    def members(step):
        return [step // chunks * GROUP + g for g in range(GROUP)], step % chunks

    def set_target(block, u, lanes, base, to):
        label = row(block, label_at(u)) - base
        pairs = []
        for t in range(trees):
            weight, node = row(block, weight_at(t, u)), row(block, node_at(t, u))
            pairs += [jnp.where(node == n, weight, 0.0) for n in range(NODES)]
        pairs = jnp.concatenate(pairs, axis=0)
        for c in range(0, SPAN, 2):
            two = [jnp.where(label == c + more, pairs, 0.0) for more in range(2)]
            to[c * depth : (c + 2) * depth, lanes] = jnp.concatenate(two, axis=0).astype(BF16)

    def set_limits(step):
        held, u = members(step)
        labels = jnp.concatenate([row(block, label_at(u)) for block in held], axis=0)
        low[step] = jnp.min(labels).astype(jnp.int32)
        high[step] = jnp.max(labels).astype(jnp.int32)

    def prepare(step, g):
        held, u = members(step)
        lanes = slice(g * LANES, (g + 1) * LANES)
        set_target(held[g], u, lanes, low[step].astype(F32), target.at[step])
        tile = jnp.concatenate([row(held[g], feature_at(f, u)) for f in range(own)], axis=0)
        tile = jnp.concatenate([tile] * copies, axis=0)
        spread[step, lanes, :] = tile.T.astype(BF16)

    bins = (first_bin + jnp.floor(iota((GROUP * LANES, LANES), 1) * (1.0 / own))).astype(BF16)
    one, zero = jnp.ones((), BF16), jnp.zeros((), BF16)

    def add(step, start, held, beside=None):
        start = pl.multiple_of(start * depth, 8)
        for at, first in enumerate(firsts):
            last = min(first + 2, tiles)
            below = [
                jnp.minimum(jnp.maximum((bins + float(tile * copies + 1)) - spread[step], zero), one)
                for tile in range(first, last)
            ]
            lanes = slice(first * LANES, last * LANES)
            total[pl.ds(start, SPAN * depth), lanes] += jnp.dot(
                held[...], jnp.concatenate(below, axis=1), preferred_element_type=F32
            )
            if beside is not None:
                beside(at)

    def more(step, carry):
        def one_pass(p, inner):
            base = low[step] + p * SPAN
            held, u = members(step)
            for g in range(GROUP):
                lanes = slice(g * LANES, (g + 1) * LANES)
                set_target(held[g], u, lanes, base.astype(F32), target.at[steps])
            add(step, base, target.at[steps])
            return inner

        return lax.fori_loop(1, (high[step] - low[step]) // SPAN + 1, one_pass, carry)

    def window(step, carry):
        set_limits(step)
        for g in range(GROUP):
            prepare(step, g)
        add(step, low[step], target.at[step])
        return carry

    def ratio(squares, sums):
        return squares / jnp.maximum(sums, 1.0)

    zeros = jnp.zeros((depth, LANES), F32)

    def set_whole():
        sums, squares = zeros, zeros
        for c in range(C):
            part = jnp.broadcast_to(total[c * depth : (c + 1) * depth, tiles * LANES - 1 :], (depth, LANES))
            whole[c * depth : (c + 1) * depth, :] = part
            sums, squares = sums + part, squares + part * part
        return ratio(squares, sums)

    def gain_of(tile, whole_ratio):
        left_sum, right_sum, left_square, right_square = zeros, zeros, zeros, zeros
        for c in range(C):
            left = total[c * depth : (c + 1) * depth, tile * LANES : (tile + 1) * LANES]
            right = whole[c * depth : (c + 1) * depth, :] - left
            left_sum, left_square = left_sum + left, left_square + left * left
            right_sum, right_square = right_sum + right, right_square + right * right
        return ratio(left_square, left_sum) + ratio(right_square, right_sum) - whole_ratio

    found = []
    if steps <= UNROLLED:
        for step in range(min(2, steps)):
            set_limits(step)
        for g in range(GROUP):
            prepare(0, g)
        for step in range(steps - 1):

            def prepare_next(at, step=step):
                if at == 0 and step + 2 < steps:
                    set_limits(step + 2)
                for g in range(at, GROUP, len(firsts)):
                    prepare(step + 1, g)

            add(step, low[step], target.at[step], prepare_next)
        lax.fori_loop(0, steps, more, 0)
        ratios = []

        def score_done(at):
            if at == 0:
                ratios.append(set_whole())
            else:
                first = firsts[at - 1]
                found.extend(gain_of(tile, ratios[0]) for tile in range(first, min(first + 2, tiles)))

        add(steps - 1, low[steps - 1], target.at[steps - 1], score_done)
        score_done(len(firsts))
    else:
        lax.fori_loop(0, steps, window, 0)
        lax.fori_loop(0, steps, more, 0)
        whole_ratio = set_whole()
        found.extend(gain_of(tile, whole_ratio) for tile in range(tiles))
    best = functools.reduce(jnp.maximum, found)
    shift = own
    while shift < LANES:
        best = jnp.maximum(best, pltpu.roll(best, shift, 1))
        shift *= 2
    if not direct:
        gain_ref[...] = best[:, :own]
        return
    piece = own // trees
    me = lax.axis_index("leaf")
    lane = lax.broadcasted_iota(jnp.int32, (depth, LANES), 1)
    sent = best
    for leaf in range(trees):
        moved = pltpu.roll(best, lax.rem((me - leaf) * piece + LANES, LANES), 1)
        sent = jnp.where(lane // own % trees == leaf, moved, sent)
    for t in range(trees):
        line = jnp.where(lane[:1] < trees * own, sent[t * NODES : t * NODES + 1], sent[t * NODES + 1 : t * NODES + 2])
        for block in range(blocks):
            gain_ref[block * trees + t] = line


def finish_kernel(blocks, trees, own, msg_ref, gain_ref, best_ref):
    here = block_of_device()
    piece = own // trees
    half = trees * own
    lane = lax.broadcasted_iota(jnp.int32, (1, LANES), 1)
    mine = msg_ref[here * trees]
    for leaf in range(1, trees):
        mine = jnp.where(lane // piece % trees == leaf, msg_ref[here * trees + leaf], mine)
    chains = [
        functools.reduce(jnp.maximum, [msg_ref[block * trees + leaf] for block in range(blocks)]) for leaf in range(trees)
    ]
    top = functools.reduce(jnp.maximum, chains)
    for n in range(NODES):
        gain_ref[0, n : n + 1, :] = mine[:, n * half : (n + 1) * half]
        best_ref[:, n : n + 1] = jnp.max(top[:, n * half : (n + 1) * half], axis=1, keepdims=True)


def score(message, places, sizes, direct):
    blocks, chunks, trees, own = sizes
    depth = trees * NODES
    steps = blocks * chunks // GROUP
    columns = -(-(HIGHEST + 1 - LOWEST) * own // LANES) * LANES
    return pl.pallas_call(
        functools.partial(score_kernel, places, sizes, direct),
        out_shape=jax.ShapeDtypeStruct((blocks * trees, 1, LANES) if direct else (depth, own), F32),
        in_specs=[VMEM],
        out_specs=VMEM,
        scratch_shapes=[
            pltpu.VMEM(message.shape, F32),
            pltpu.VMEM((steps + 1, SPAN * depth, GROUP * LANES), BF16),
            pltpu.VMEM((steps, GROUP * LANES, LANES), BF16),
            pltpu.VMEM(((C + SPAN) * depth, columns), F32),
            pltpu.VMEM((C * depth, LANES), F32),
            pltpu.SMEM((steps,), jnp.int32),
            pltpu.SMEM((steps,), jnp.int32),
        ],
        compiler_params=pltpu.CompilerParams(vmem_limit_bytes=40 << 20),
    )(message)


def local(features, labels, weights, nodes, *, blocks, trees):
    feature_total, rows = features.shape
    own = feature_total // (blocks * trees)
    devices = blocks * trees
    chunks = rows // LANES
    split_features = own % trees == 0
    if split_features:
        piece = own // trees
        deep = (piece + 3) * chunks
        held = devices * piece
        message = pl.pallas_call(
            functools.partial(sort_kernel, (blocks, trees, own, rows, chunks, piece)),
            out_shape=jax.ShapeDtypeStruct((devices, deep, LANES), BF16),
            in_specs=[
                HBM,
                HBM,
                HBM,
                HBM,
            ],
            out_specs=VMEM,
            scratch_shapes=[
                pltpu.VMEM((blocks, own, rows), F32),
                pltpu.VMEM((1, rows), jnp.int32),
                pltpu.VMEM((1, rows), BF16),
                pltpu.VMEM((1, rows), jnp.int32),
                pltpu.VMEM((held + 16, rows), BF16),
                pltpu.VMEM((chunks, held + 16, LANES), F32),
                pltpu.VMEM(((devices + 1) * deep, LANES), F32),
                pltpu.SemaphoreType.DMA((4,)),
            ],
            compiler_params=pltpu.CompilerParams(vmem_limit_bytes=60 << 20),
        )(features.reshape(blocks, trees, own, rows), labels.reshape(1, rows), weights, nodes)
        message = lax.all_to_all(message, ALL, 0, 0, tiled=True)
        message = message.reshape(blocks, trees, deep, LANES)
        places = (
            lambda f, u: (f // piece, (f % piece) * chunks + u),
            lambda t, u: (t, piece * chunks + u),
            lambda t, u: (t, (piece + 1) * chunks + u),
            lambda u: (0, (piece + 2) * chunks + u),
        )
    else:
        share = rows // trees
        mine = lax.dynamic_slice_in_dim(features, lax.axis_index("leaf") * share, share, 1)
        binned = bin_index(mine).astype(BF16).reshape(devices, own * share)
        quarter = lax.dynamic_slice_in_dim(labels, lax.axis_index("leaf") * share, share, 0)
        common = jnp.concatenate([weights[0], nodes[0].astype(BF16), quarter.astype(BF16)])
        message = jnp.concatenate([binned, jnp.broadcast_to(common, (devices, common.shape[0]))], axis=1)
        message = lax.all_to_all(message, ALL, 0, 0, tiled=True).reshape(blocks, trees, -1)
        ends = (own * share, own * share + rows, own * share + 2 * rows)
        parts = [
            message[:, :, : ends[0]].reshape(blocks, trees, own, share).transpose(0, 2, 1, 3),
            message[:, :, ends[0] : ends[1]],
            message[:, :, ends[1] : ends[2]],
            message[:, :, ends[2] :],
        ]
        message = jnp.concatenate([p.reshape(blocks, -1, LANES) for p in parts], axis=1)[:, None]
        places = (
            lambda f, u: (0, f * chunks + u),
            lambda t, u: (0, (own + t) * chunks + u),
            lambda t, u: (0, (own + trees + t) * chunks + u),
            lambda u: (0, (own + 2 * trees) * chunks + u),
        )
    sizes = (blocks, chunks, trees, own)
    direct = split_features and NODES * trees * own == LANES
    gains = score(message, places, sizes, direct)
    if direct:
        return pl.pallas_call(
            functools.partial(finish_kernel, blocks, trees, own),
            out_shape=(
                jax.ShapeDtypeStruct((1, NODES, trees * own), F32),
                jax.ShapeDtypeStruct((1, NODES), F32),
            ),
            in_specs=[VMEM],
            out_specs=(pl.BlockSpec(), pl.BlockSpec()),
        )(lax.all_to_all(gains, ALL, 0, 0, tiled=True))
    outgoing = jnp.broadcast_to(gains.reshape(1, trees, NODES * own), (blocks, trees, NODES * own))
    scores = lax.all_to_all(outgoing.reshape(devices, NODES * own), ALL, 0, 0, tiled=True)
    scores = scores.reshape(blocks, trees, NODES, own)
    block = lax.dynamic_index_in_dim(scores, block_of_device(), 0, keepdims=False)
    if split_features:
        split_gain = block.reshape(trees, NODES, trees, own // trees).transpose(1, 2, 0, 3)
    else:
        split_gain = block.transpose(1, 0, 2)
    return split_gain.reshape(1, NODES, trees * own), jnp.max(scores, axis=(0, 1, 3)).reshape(1, NODES)


def solution(mesh):
    shape = mesh.shape
    return jax.shard_map(
        functools.partial(local, blocks=shape["rows"] * shape["feat"], trees=shape["leaf"]),
        mesh=mesh,
        in_specs=(
            P(None, ("rows", "feat")),
            P(("rows", "feat")),
            P("leaf", ("rows", "feat")),
            P("leaf", ("rows", "feat")),
        ),
        out_specs=(P("leaf", None, ("rows", "feat")), P("leaf", None)),
        check_vma=False,
    )
```
